256 devices in a mesh: region: 32 (over y, z), group: 8 (over x, core).
Axes of the slice: x: 4, y: 4, z: 8, core: 2. Of those that a mesh axis runs over, the one named last changes fastest.
Arguments:
- points: bfloat16 [8, 8192, 512], P('group', 'region'), may hold values from -60 to 60
- row_slot: int32 [8, 8192], P('group', 'region'), may hold values from 0 to 511, as said below
- pos_slot: int32 [8, 8192], P('group', 'region'), may hold values from 0 to 511, as said below
- patch_ids: int32 [8, 32, 256], P('group', 'region'), may hold values from 0 to 3, as said below
- bn_gain: float32 [512], replicated, may hold values from 0.1 to 1.9
- bn_bias: float32 [512], replicated, may hold values from -3 to 3
- w_qkv: bfloat16 [512, 1536], replicated, may hold values from -0.25 to 0.25
- w_proj: bfloat16 [512, 512], replicated, may hold values from -1.5 to 1.5
- cotangent: bfloat16 [8, 8192, 512], P('group', 'region'), may hold values from -2 to 2
Outputs:
- output: bfloat16 [8, 8192, 512], P('group', 'region')
- grad_points: bfloat16 [8, 8192, 512], P('group', 'region')
- grad_w_qkv: float32 [512, 1536], P('group', 'region')
- grad_w_proj: float32 [512, 512], P('group', 'region')
- grad_gain: float32 [512], replicated
- grad_bias: float32 [512], replicated
The draws below stay inside these ranges and needn't reach their ends.
Inputs may be any that keep to these rules, and one draw needn't show every extreme that they name: Values of one device's 256 points are distinct; row_slot // 16 is the destination range and row_slot % 16 the slot within it. Each device sends at most 16 points to one range, and in every window some device sends exactly 16 to some range. Values of one range's 256 positions are distinct; pos_slot // 16 is the source brick and pos_slot % 16 the slot it used, so row_slot and pos_slot describe one bijection between brick and serialized positions of a window, and every range receives exactly 256 points. `patch_ids`: ids count patches within one device's range of 256 serialized positions, never falling along it; a patch never leaves that range and holds at most 256 positions, and in every window some patch holds exactly 256.
All inputs are finite; a program needn't handle non-finite values.
Results may differ from the reference program's by a relative error of at most 0.025.
Values may be sent and summed in bfloat16 or wider, within the bound.
A program may use at most 64 MiB of HBM per device.

```python
import jax
import jax.numpy as jnp
from jax import lax

WIDTH = 512
HEADS = 32
PTS_DEV = 256
HEAD_DIM = 16
RANGES = 32
WINDOWS = 8
WIN_PTS = 8192
TOTAL = 65536
CAP = 16
LONGEST = 256


def route_plan(key):
    plan_key = jax.random.fold_in(key, 101)

    def one_window(window):
        window_key = jax.random.fold_in(plan_key, window)
        order_key, size_key = jax.random.split(window_key)
        offset_order = jax.random.permutation(order_key, RANGES)
        extra = jax.random.randint(size_key, (RANGES // 2,), 0, CAP // 2 + 1)
        extra = extra.at[0].set(CAP // 2)
        counts = jnp.zeros((RANGES,), jnp.int32)
        counts = counts.at[offset_order[0::2]].set(CAP // 2 + extra)
        counts = counts.at[offset_order[1::2]].set(CAP // 2 - extra)
        ends = jnp.cumsum(counts).astype(jnp.int32)
        rank_index = jnp.arange(PTS_DEV, dtype=jnp.int32)
        offset_of = jnp.sum((rank_index[:, None] >= ends[None, :]).astype(jnp.int32), axis=1)
        within = rank_index - (ends - counts)[offset_of]
        return (offset_of, within)
    return jax.vmap(one_window)(jnp.arange(WINDOWS, dtype=jnp.int32))


def draw_row_slot(key, part):
    offset_of, within = route_plan(key)
    key = jax.random.fold_in(key, 7)

    def one_device(window, source):
        device_key = jax.random.fold_in(jax.random.fold_in(key, window), source)
        row_order = jax.random.permutation(device_key, PTS_DEV)
        target = (source + offset_of[window]) % RANGES
        slot_value = target * CAP + within[window]
        return jnp.zeros((PTS_DEV,), jnp.int32).at[row_order].set(slot_value)
    windows = jnp.arange(WINDOWS, dtype=jnp.int32)
    sources = jnp.arange(RANGES, dtype=jnp.int32)
    table = jax.vmap(lambda window: jax.vmap(lambda source: one_device(window, source))(sources))(windows)
    return table.reshape(WINDOWS, WIN_PTS)


def draw_pos_slot(key, part):
    offset_of, within = route_plan(key)
    key = jax.random.fold_in(key, 9)

    def one_device(window, target):
        device_key = jax.random.fold_in(jax.random.fold_in(key, window), target)
        pos_order = jax.random.permutation(device_key, PTS_DEV)
        source = (target - offset_of[window]) % RANGES
        slot_value = source * CAP + within[window]
        return jnp.zeros((PTS_DEV,), jnp.int32).at[pos_order].set(slot_value)
    windows = jnp.arange(WINDOWS, dtype=jnp.int32)
    targets = jnp.arange(RANGES, dtype=jnp.int32)
    table = jax.vmap(lambda window: jax.vmap(lambda target: one_device(window, target))(targets))(windows)
    return table.reshape(WINDOWS, WIN_PTS)


def draw_patch_ids(key, part):
    key = jax.random.fold_in(key, 13)
    position = jnp.arange(PTS_DEV, dtype=jnp.int32)
    on_grid = position % LONGEST == 0

    def one_range(range_key, cuts):
        shuffled = jax.random.permutation(range_key, PTS_DEV).astype(jnp.int32)
        rank_of = jnp.zeros((PTS_DEV,), jnp.int32).at[shuffled].set(position)
        score = jnp.where(on_grid, 2 * PTS_DEV, rank_of).astype(jnp.int32)
        ordered = jnp.argsort(score, stable=True).astype(jnp.int32)
        chosen_rank = jnp.zeros((PTS_DEV,), jnp.int32).at[ordered].set(position)
        is_cut = jnp.logical_and(chosen_rank < cuts, jnp.logical_not(on_grid))
        starts = jnp.logical_or(jnp.logical_and(on_grid, position > 0), is_cut)
        return jnp.cumsum(starts.astype(jnp.int32)).astype(jnp.int32)

    def one_window(window):
        window_key = jax.random.fold_in(key, window)
        pick_key, cut_key = jax.random.split(window_key)
        picked = jax.random.permutation(pick_key, RANGES)
        cut_counts = jax.random.randint(cut_key, (RANGES,), 0, 4).astype(jnp.int32)
        cut_counts = cut_counts.at[picked[0]].set(0).at[picked[1]].set(3)
        ranges = jnp.arange(RANGES, dtype=jnp.int32)
        return jax.vmap(lambda index, cuts: one_range(jax.random.fold_in(window_key, 1000 + index), cuts))(ranges, cut_counts)
    return jax.vmap(one_window)(jnp.arange(WINDOWS, dtype=jnp.int32))


def draw_points(key, part):
    key = jax.random.fold_in(key, 3)
    base_key, row_key, col_key = jax.random.split(key, 3)
    shape = (WINDOWS, WIN_PTS, WIDTH)
    along = jnp.arange(WIN_PTS, dtype=jnp.float32) / WIN_PTS
    by_window = jnp.arange(WINDOWS, dtype=jnp.float32) / WINDOWS
    rising = (1.0 + 2.0 * along)[None, :, None] * (1.0 + by_window)[:, None, None]
    col_scale = jnp.exp(jax.random.uniform(col_key, (1, 1, WIDTH), minval=-1.2, maxval=1.2))
    base = jnp.clip(jax.random.normal(base_key, shape), -4.0, 4.0)
    row_scale = jnp.exp(jax.random.uniform(row_key, (WINDOWS, WIN_PTS, 1), minval=-1.2, maxval=1.2))
    values_f = base * row_scale * col_scale * rising
    return jnp.clip(values_f, -60.0, 60.0).astype(jnp.bfloat16)


def strengthened(array, stream_key, source, target, shards_of, factor):
    owner, partner = [(jnp.arange(array.shape[dim]) // (array.shape[dim] // shards_of)).reshape([-1 if axis == dim else 1 for axis in range(array.ndim)]) for dim in (source, target)]
    chosen = jax.random.permutation(stream_key, shards_of)[partner]
    strong = (owner == chosen) | (owner == (partner + shards_of // 2) % shards_of)
    return jnp.where(strong, factor * array, array)


def block_scale(own_key, shape, shards, smallest, top_value):
    def one(dim, blocks):
        steps = jax.random.uniform(jax.random.fold_in(jax.random.fold_in(own_key, 6), dim), (blocks,), jnp.float32, smallest / len(shards), top_value / len(shards))
        return jnp.repeat(jnp.exp(steps), shape[dim] // blocks).reshape((-1,) + (1,) * (len(shape) - dim - 1))

    loudness = one(*shards[0])
    for cut in shards[1:]:
        loudness = loudness * one(*cut)
    return loudness


def scatter_about(stream_key, dims, scale, bound, cuts=(), held_as=jnp.bfloat16):
    level = block_scale(stream_key, dims, cuts, -0.22, 0.18) if cuts else 1.0
    entries = jax.random.normal(stream_key, dims, jnp.float32) * scale * level
    return jnp.minimum(jnp.maximum(entries, -bound), bound).astype(held_as)


def noise_with(stream_key, shape, scale, most, pieces, heavy, kind=jnp.bfloat16):
    drawn = scale * jax.random.normal(stream_key, shape, jnp.float32)
    if pieces:
        drawn = drawn * block_scale(stream_key, shape, pieces, -0.22, 0.18)
    return jnp.clip(strengthened(drawn, jax.random.fold_in(stream_key, 3), *heavy), -most, most).astype(kind)


def setup_inputs(seed: int = 0) -> dict:
    key_list = jax.random.split(jax.random.key(seed), 10)
    return {
        "points": draw_points(jax.random.fold_in(key_list[9], 71), 0),
        "row_slot": draw_row_slot(jax.random.fold_in(key_list[9], 71), 0),
        "pos_slot": draw_pos_slot(jax.random.fold_in(key_list[9], 71), 0),
        "patch_ids": draw_patch_ids(jax.random.fold_in(key_list[9], 71), 0),
        "bn_gain": jnp.clip(1.0 + 0.18 * jax.random.normal(key_list[4], (WIDTH,), jnp.float32), 0.1, 1.9),
        "bn_bias": scatter_about(key_list[5], (WIDTH,), 0.5, 3.0, (), jnp.float32),
        "w_qkv": scatter_about(key_list[6], (WIDTH, 3 * WIDTH), WIDTH ** -0.5, 0.25),
        "w_proj": scatter_about(key_list[7], (WIDTH, WIDTH), (WIDTH // 32) ** -0.5, 1.5),
        "cotangent": noise_with(key_list[8], (WINDOWS, WIN_PTS, WIDTH), 0.3, 2.0, ((0, 8), (1, 32)), (1, 2, 32, 2.75)),
    }


EPS = 1e-05

def masked_softmax(scores, in_patch):
    scores = jnp.where(in_patch[None], scores, -1e+30)
    highest = lax.optimization_barrier(jnp.max(scores, axis=-1, keepdims=True))
    raised = jnp.exp(scores - highest)
    return raised / lax.optimization_barrier(jnp.sum(raised, axis=-1, keepdims=True))

def head_split(source, first_col):
    return source[:, first_col:first_col + WIDTH].astype(jnp.float32).reshape(source.shape[0], HEADS, HEAD_DIM)

def range_probs(qkv_rows, patch_row):
    query_f = head_split(qkv_rows, 0)
    key_f = head_split(qkv_rows, WIDTH)
    value_f = head_split(qkv_rows, 2 * WIDTH)
    in_patch = patch_row[:, None] == patch_row[None, :]
    probs = masked_softmax(jnp.einsum('qhd,khd->hqk', query_f, key_f) * HEAD_DIM ** (-0.5), in_patch)
    weights = lax.optimization_barrier(probs.astype(jnp.bfloat16)).astype(jnp.float32)
    return (query_f, key_f, value_f, probs, weights)

def range_forward(qkv_rows, patch_row):
    query_f, key_f, value_f, probs, weights = range_probs(qkv_rows, patch_row)
    mixed = jnp.einsum('hqk,khd->qhd', weights, value_f)
    return mixed.reshape(qkv_rows.shape[0], WIDTH).astype(jnp.bfloat16)

def range_backward(qkv_rows, patch_row, grad_mixed):
    query_f, key_f, value_f, probs, weights = range_probs(qkv_rows, patch_row)
    row_count = qkv_rows.shape[0]
    grad_f = grad_mixed.astype(jnp.float32).reshape(row_count, HEADS, HEAD_DIM)
    grad_weights = jnp.einsum('qhd,khd->hqk', grad_f, value_f)
    grad_values = jnp.einsum('hqk,qhd->khd', weights, grad_f)
    grad_scores = probs * (grad_weights - lax.optimization_barrier(jnp.sum(probs * grad_weights, axis=-1, keepdims=True)))
    grad_scores = lax.optimization_barrier(grad_scores.astype(jnp.bfloat16)).astype(jnp.float32)
    grad_queries = jnp.einsum('hqk,khd->qhd', grad_scores, key_f) * HEAD_DIM ** (-0.5)
    grad_keys = jnp.einsum('hqk,qhd->khd', grad_scores, query_f) * HEAD_DIM ** (-0.5)
    joined = jnp.concatenate([grad_queries.reshape(row_count, WIDTH), grad_keys.reshape(row_count, WIDTH), grad_values.reshape(row_count, WIDTH)], axis=1)
    return joined.astype(jnp.bfloat16)

def window_pass(normed_w, grad_w, row_w, pos_w, patch_w, w_qkv, w_proj):
    point_index = jnp.arange(WIN_PTS, dtype=jnp.int32)
    home_range = point_index // PTS_DEV
    table_pos = row_w // CAP * RANGES + home_range
    lookup = jnp.zeros((RANGES * RANGES * CAP,), jnp.int32).at[table_pos * CAP + row_w % CAP].set(point_index)
    serial_pos = (home_range * RANGES + pos_w // CAP) * CAP + pos_w % CAP
    order = lookup[serial_pos].astype(jnp.int32)
    serial = normed_w[order]
    qkv_rows = jnp.dot(serial, w_qkv, preferred_element_type=jnp.float32).astype(jnp.bfloat16)
    qkv_ranges = qkv_rows.reshape(RANGES, PTS_DEV, 3 * WIDTH)
    mixed = lax.map(lambda item: range_forward(item[0], item[1]), (qkv_ranges, patch_w)).reshape(WIN_PTS, WIDTH)
    branch = jnp.dot(mixed, w_proj, preferred_element_type=jnp.float32).astype(jnp.bfloat16)
    output = jnp.zeros((WIN_PTS, WIDTH), jnp.bfloat16).at[order].set(branch)
    grad_serial = grad_w[order]
    proj_grad = jnp.dot(mixed.T, grad_serial, preferred_element_type=jnp.float32)
    grad_mixed = jnp.dot(grad_serial, w_proj.T, preferred_element_type=jnp.float32).astype(jnp.bfloat16)
    grad_qkv = lax.map(lambda item: range_backward(item[0], item[1], item[2]), (qkv_ranges, patch_w, grad_mixed.reshape(RANGES, PTS_DEV, WIDTH))).reshape(WIN_PTS, 3 * WIDTH)
    qkv_grad = jnp.dot(serial.T, grad_qkv, preferred_element_type=jnp.float32)
    grad_in = jnp.dot(grad_qkv, w_qkv.T, preferred_element_type=jnp.float32).astype(jnp.bfloat16)
    grad_normed = jnp.zeros((WIN_PTS, WIDTH), jnp.bfloat16).at[order].set(grad_in)
    return (output, grad_normed, qkv_grad, proj_grad)

def reference(points, row_slot, pos_slot, patch_ids, bn_gain, bn_bias, w_qkv, w_proj, cotangent):
    values_f = points.astype(jnp.float32)
    mean_all = lax.optimization_barrier(jnp.sum(values_f, axis=(0, 1))) / TOTAL
    centered = values_f - mean_all
    spread = lax.optimization_barrier(jnp.sum(centered * centered, axis=(0, 1))) / TOTAL
    inv_std = lax.rsqrt(spread + EPS)
    unit_rows = centered * inv_std
    normed = (unit_rows * bn_gain + bn_bias).astype(jnp.bfloat16)
    output, grad_normed, qkv_grads, proj_grads = lax.map(lambda item: window_pass(item[0], item[1], item[2], item[3], item[4], w_qkv, w_proj), (normed, cotangent, row_slot, pos_slot, patch_ids))
    grad_w_qkv = lax.optimization_barrier(jnp.sum(qkv_grads, axis=0))
    grad_w_proj = lax.optimization_barrier(jnp.sum(proj_grads, axis=0))
    grad_f = grad_normed.astype(jnp.float32)
    grad_bias = lax.optimization_barrier(jnp.sum(grad_f, axis=(0, 1)))
    grad_gain = lax.optimization_barrier(jnp.sum(grad_f * unit_rows, axis=(0, 1)))
    grad_points = inv_std * (grad_f * bn_gain - bn_gain * grad_bias / TOTAL - unit_rows * (bn_gain * grad_gain / TOTAL))
    return (output, grad_points.astype(jnp.bfloat16), grad_w_qkv, grad_w_proj, grad_gain, grad_bias)
```

```python
import functools

import jax
import jax.numpy as jnp
from jax import lax
from jax.experimental import pallas as pl
from jax.experimental.pallas import tpu as pltpu
from jax.sharding import PartitionSpec as P

HEAD_DIM = 16
EPS = 1e-05
PTS = 256
WIDTH = 512
CAP = 16
REGIONS = 32
GROUPS = 8
TOTAL = 65536
MESH = pl.DeviceIdType.MESH
BF = jnp.bfloat16
F32 = jnp.float32


def dot_nn(a, b):
    return jnp.dot(a, b, preferred_element_type=F32)


def dot_nt(a, b):
    return lax.dot_general(a, b, (((1,), (1,)), ((), ())), preferred_element_type=F32)


def as_column(row):
    return jnp.broadcast_to(row, (128, row.shape[1])).T


def slot_rows(row):
    slots = lax.broadcasted_iota(jnp.int32, (REGIONS * CAP, PTS), 0)
    return jnp.where(slots == row, 1.0, 0.0).astype(BF)


def slot_columns(row):
    col = as_column(row.astype(F32)).astype(jnp.int32)
    lane = lax.broadcasted_iota(jnp.int32, (PTS, 128), 1)
    parts = [jnp.where(col == lane + 128 * j, 1.0, 0.0) for j in range(4)]
    return jnp.concatenate(parts, axis=1).astype(BF)


def store_rows(ref, at, first, row):
    for j in range(4):
        ref[at, first + j : first + j + 1, :] = row[:, 128 * j : 128 * (j + 1)]


def load_row(block, first):
    return jnp.concatenate([block[first + j : first + j + 1, :] for j in range(4)], axis=1)


def kernel(
    x_ref, rs_ref, ps_ref, pid_ref, gain_ref, bias_ref, wqkv_hbm, wproj_hbm, cot_ref,
    out_ref, gp_ref, gwq_ref, gwp_ref, gg_ref, gb_ref,
    wqkv, wproj, w_sem,
    send_a, recv_a, send_b, recv_b, send_c, recv_c, send_d, recv_d,
    st1, st2, gs1, gs2,
    p_t, q_n, q_t, patch_bias,
    unit_s, serial, qkv, qs, kt, vt, probs, mixed_t, mixed,
    g_serial_t, gm, big_w, big_d, stack_g, stack_q, gqkv, gqkv_t,
    g32, g_core, r_core, s_x, r_x, s_r, r_r, fin, fin_t,
    send_sems, recv_sems,
):
    r = lax.axis_index("region")
    g = lax.axis_index("group")
    xx = g // 2
    core = g % 2

    def each_region(act):
        def body(k, carry):
            act(lax.rem(r + k, REGIONS))
            return carry

        lax.fori_loop(1, REGIONS, body, 0)

    def each_group(act):
        def body(k, carry):
            act(lax.rem(g + k, GROUPS))
            return carry

        lax.fori_loop(1, GROUPS, body, 0)

    def send(src, dst, stage, to):
        pltpu.make_async_remote_copy(
            src_ref=src, dst_ref=dst, send_sem=send_sems.at[stage], recv_sem=recv_sems.at[stage],
            device_id=to, device_id_type=MESH,
        ).start()

    def wait(ref, sem):
        pltpu.make_async_copy(ref, ref, sem).wait()

    barrier = pltpu.get_barrier_semaphore()
    each_region(
        lambda p: pl.semaphore_signal(barrier, inc=1, device_id=(p, g), device_id_type=MESH)
    )
    each_group(
        lambda p: pl.semaphore_signal(barrier, inc=1, device_id=(r, p), device_id_type=MESH)
    )
    load_qkv = pltpu.make_async_copy(wqkv_hbm, wqkv, w_sem.at[0])
    load_proj = pltpu.make_async_copy(wproj_hbm, wproj, w_sem.at[1])
    load_qkv.start()
    load_proj.start()

    x = x_ref[...]
    xf = x.astype(F32)
    mean_l = jnp.sum(xf, axis=0, keepdims=True) * (1.0 / PTS)
    dev = xf - mean_l
    store_rows(st1, g, 0, mean_l)
    store_rows(st1, g, 4, jnp.sum(dev * dev, axis=0, keepdims=True))
    p_n = slot_rows(rs_ref[...])
    send_a[...] = dot_nn(p_n, x).astype(BF).reshape(REGIONS, CAP, WIDTH)

    pl.semaphore_wait(barrier, REGIONS - 1 + GROUPS - 1)

    each_group(lambda p: send(st1.at[g], st1.at[g], 0, (r, p)))
    each_region(lambda p: send(send_a.at[p], recv_a.at[r], 1, (p, g)))
    recv_a[r] = send_a[r]

    send_b[...] = dot_nn(p_n, cot_ref[...]).astype(BF).reshape(REGIONS, CAP, WIDTH)
    p_t[...] = slot_columns(rs_ref[...])
    q_n[...] = slot_rows(ps_ref[...])
    q_t[...] = slot_columns(ps_ref[...])
    pid_row = pid_ref[...]
    pid_col = as_column(pid_row.astype(F32)).astype(jnp.int32)
    patch_bias[...] = jnp.concatenate(
        [
            jnp.where(pid_col == pid_row[:, 128 * j : 128 * (j + 1)], 0.0, -1e30)
            for j in range(2)
        ],
        axis=1,
    )

    wait(st1.at[pl.ds(0, GROUPS - 1)], recv_sems.at[0])

    def merge(block, count, each):
        means, squares = block[:, 0:4, :], block[:, 4:8, :]
        mean = jnp.sum(means, axis=0) * (1.0 / count)
        off = means - mean[None]
        return mean, jnp.sum(squares, axis=0) + each * jnp.sum(off * off, axis=0)

    mean_g, square_g = merge(st1[...], GROUPS, float(PTS))
    st2[r, 0:4, :] = mean_g
    st2[r, 4:8, :] = square_g
    each_region(lambda p: send(st2.at[r], st2.at[r], 2, (p, g)))

    each_region(lambda p: send(send_b.at[p], recv_b.at[r], 3, (p, g)))
    recv_b[r] = send_b[r]

    wait(st2.at[pl.ds(0, REGIONS - 1)], recv_sems.at[2])
    mean_4, square_4 = merge(st2[...], REGIONS, float(PTS * GROUPS))
    inv_4 = lax.rsqrt(square_4 * (1.0 / TOTAL) + EPS)
    mean_all = load_row(mean_4, 0)
    inv_std = load_row(inv_4, 0)
    gain = gain_ref[...]

    wait(recv_a.at[pl.ds(0, REGIONS - 1)], recv_sems.at[1])
    pts = dot_nn(q_t[...], recv_a[...].reshape(REGIONS * CAP, WIDTH))
    unit = (pts - mean_all) * inv_std
    unit_s[...] = unit
    serial[...] = (unit * gain + bias_ref[...]).astype(BF)

    load_qkv.wait()
    load_proj.wait()
    qkv[...] = dot_nn(serial[...], wqkv[...]).astype(BF)
    qs[...] = qkv[:, 0:WIDTH] * jnp.asarray(0.25, BF)
    kt[...] = qkv[:, WIDTH : 2 * WIDTH].T
    vt[...] = qkv[:, 2 * WIDTH : 3 * WIDTH].T

    lane_head = lax.broadcasted_iota(jnp.int32, (1, 128), 1) // HEAD_DIM

    def head_mask(h):
        return jnp.where(lane_head == h, 1.0, 0.0).astype(BF)

    def forward(chunk, carry):
        col = pl.multiple_of(chunk * 128, 128)
        keys = qkv[:, pl.ds(WIDTH + col, 128)]
        queries = qs[:, pl.ds(col, 128)]
        for h in range(8):
            scores = dot_nt(keys * head_mask(h), queries) + patch_bias[...]
            raised = jnp.exp(scores - jnp.max(scores, axis=0, keepdims=True))
            p = raised * (1.0 / jnp.sum(raised, axis=0, keepdims=True))
            probs[chunk * 8 + h] = p
            rows = pl.ds(pl.multiple_of(col + HEAD_DIM * h, HEAD_DIM), HEAD_DIM)
            mixed_t[rows, :] = dot_nn(vt[rows, :], p.astype(BF)).astype(BF)
        return carry

    lax.fori_loop(0, 4, forward, 0)
    mixed[...] = mixed_t[...].T
    branch = dot_nn(mixed[...], wproj[...]).astype(BF)
    send_c[...] = dot_nn(q_n[...], branch).astype(BF).reshape(REGIONS, CAP, WIDTH)
    each_region(lambda p: send(send_c.at[p], recv_c.at[r], 4, (p, g)))
    recv_c[r] = send_c[r]

    wait(recv_b.at[pl.ds(0, REGIONS - 1)], recv_sems.at[3])
    g_serial = dot_nn(q_t[...], recv_b[...].reshape(REGIONS * CAP, WIDTH)).astype(BF)
    g_serial_t[...] = g_serial.T
    gm[...] = dot_nt(g_serial, wproj[...]).astype(BF)

    def backward(chunk, carry):
        col = pl.multiple_of(chunk * 128, 128)
        values = qkv[:, pl.ds(2 * WIDTH + col, 128)]
        grads = gm[:, pl.ds(col, 128)]
        queries = qs[:, pl.ds(col, 128)]
        for h in range(8):
            mask = head_mask(h)
            span = slice(PTS * h, PTS * (h + 1))
            grad_w = dot_nt(values * mask, grads)
            p = probs[chunk * 8 + h]
            total = jnp.sum(p * grad_w, axis=0, keepdims=True)
            ds = (p * (grad_w - total)).astype(BF)
            big_w[:, span] = p.astype(BF)
            big_d[:, span] = ds
            stack_g[span, :] = grads * mask
            stack_q[span, :] = queries * mask
            rows = pl.ds(pl.multiple_of(col + HEAD_DIM * h, HEAD_DIM), HEAD_DIM)
            gqkv_t[rows, :] = (dot_nn(kt[rows, :], ds) * 0.25).astype(BF)
        gqkv[:, pl.ds(WIDTH + col, 128)] = dot_nn(big_d[...], stack_q[...]).astype(BF)
        gqkv[:, pl.ds(2 * WIDTH + col, 128)] = dot_nn(big_w[...], stack_g[...]).astype(BF)
        return carry

    lax.fori_loop(0, 4, backward, 0)
    gqkv[:, 0:WIDTH] = gqkv_t[0:WIDTH, :].T
    gqkv_t[WIDTH : 3 * WIDTH, :] = gqkv[:, WIDTH : 3 * WIDTH].T

    def weight_grads(part, carry):
        q_rows = dot_nn(gqkv_t[pl.ds(pl.multiple_of(part * 384, 384), 384), :], serial[...])
        p_rows = dot_nn(g_serial_t[pl.ds(pl.multiple_of(part * 128, 128), 128), :], mixed[...])
        for i in range(8):
            low = pl.multiple_of(part * 256 + i * 32, 32)
            for b in range(4):
                cols = slice(128 * b, 128 * (b + 1))
                g32[0, b, pl.ds(low, 32), :] = q_rows[48 * i : 48 * i + 32, cols]
                g32[1, b, pl.ds(low, 16), :] = q_rows[48 * i + 32 : 48 * i + 48, cols]
                g32[1, b, pl.ds(low + 16, 16), :] = p_rows[16 * i : 16 * i + 16, cols]
        return carry

    lax.fori_loop(0, 4, weight_grads, 0)
    g_core[...] = g32[1 - core].astype(BF)
    sibling = (r, xx * 2 + 1 - core)
    send(g_core, r_core, 5, sibling)

    grad_in = dot_nt(gqkv[...], wqkv[...]).astype(BF)
    send_d[...] = dot_nn(q_n[...], grad_in).astype(BF).reshape(REGIONS, CAP, WIDTH)
    grad_f = grad_in.astype(F32)
    store_rows(gs1, g, 0, jnp.sum(grad_f, axis=0, keepdims=True))
    store_rows(gs1, g, 4, jnp.sum(grad_f * unit_s[...], axis=0, keepdims=True))
    each_group(lambda p: send(gs1.at[g], gs1.at[g], 6, (r, p)))
    each_region(lambda p: send(send_d.at[p], recv_d.at[r], 7, (p, g)))
    recv_d[r] = send_d[r]

    wait(r_core, recv_sems.at[5])
    for b in range(4):
        s_x[b] = (g32[core, b] + r_core[b].astype(F32)).astype(BF)
    for k in range(1, 4):
        xp = lax.rem(xx + k, 4)
        send(s_x.at[xp], r_x.at[xx], 8, (r, xp * 2 + core))

    wait(gs1.at[pl.ds(0, GROUPS - 1)], recv_sems.at[6])
    gs2[r] = jnp.sum(gs1[...], axis=0)
    each_region(lambda p: send(gs2.at[r], gs2.at[r], 9, (p, g)))

    wait(recv_c.at[pl.ds(0, REGIONS - 1)], recv_sems.at[4])
    out_ref[...] = dot_nn(p_t[...], recv_c[...].reshape(REGIONS * CAP, WIDTH)).astype(BF)

    wait(r_x.at[pl.ds(0, 3)], recv_sems.at[8])
    mine = g32[core, xx] + r_core[xx].astype(F32)
    for k in range(1, 4):
        mine = mine + r_x[lax.rem(xx + k, 4)].astype(F32)
    s_r[...] = mine.astype(BF).reshape(REGIONS, 32, 128)
    each_region(lambda p: send(s_r.at[p], r_r.at[r], 10, (p, g)))
    r_r[r] = s_r[r]

    wait(gs2.at[pl.ds(0, REGIONS - 1)], recv_sems.at[9])
    sums = jnp.sum(gs2[...], axis=0)
    grad_bias = load_row(sums, 0)
    grad_gain = load_row(sums, 4)
    gb_ref[...] = grad_bias
    gg_ref[...] = grad_gain

    wait(recv_d.at[pl.ds(0, REGIONS - 1)], recv_sems.at[7])
    grad_n = dot_nn(p_t[...], recv_d[...].reshape(REGIONS * CAP, WIDTH))
    unit_b = (x_ref[...].astype(F32) - mean_all) * inv_std
    scale = 1.0 / TOTAL
    gp_ref[...] = (
        inv_std
        * (grad_n * gain - gain * grad_bias * scale - unit_b * (gain * grad_gain * scale))
    ).astype(BF)

    wait(r_r.at[pl.ds(0, REGIONS - 1)], recv_sems.at[10])
    fin[2:4] = jnp.zeros((2, 32, 128), F32)
    fin[core] = jnp.sum(r_r[...].astype(F32), axis=0)
    send(fin.at[core], fin.at[core], 11, sibling)
    wait(fin.at[0], recv_sems.at[11])
    fin_t[...] = fin[...].reshape(128, 128).T
    own = fin_t[pl.ds(pl.multiple_of(core * 64, 64), 64), :]
    gwq_ref[...] = own[:, 0:48]
    gwp_ref[...] = own[:, 48:64]

    wait(st1.at[pl.ds(0, GROUPS - 1)], send_sems.at[0])
    wait(send_a.at[pl.ds(0, REGIONS - 1)], send_sems.at[1])
    wait(st2.at[pl.ds(0, REGIONS - 1)], send_sems.at[2])
    wait(send_b.at[pl.ds(0, REGIONS - 1)], send_sems.at[3])
    wait(send_c.at[pl.ds(0, REGIONS - 1)], send_sems.at[4])
    wait(g_core, send_sems.at[5])
    wait(gs1.at[pl.ds(0, GROUPS - 1)], send_sems.at[6])
    wait(send_d.at[pl.ds(0, REGIONS - 1)], send_sems.at[7])
    wait(s_x.at[pl.ds(0, 3)], send_sems.at[8])
    wait(gs2.at[pl.ds(0, REGIONS - 1)], send_sems.at[9])
    wait(s_r.at[pl.ds(0, REGIONS - 1)], send_sems.at[10])
    wait(fin.at[0], send_sems.at[11])


def on_device(points, row_slot, pos_slot, patch_ids, bn_gain, bn_bias, w_qkv, w_proj, cotangent):
    vmem = pl.BlockSpec(memory_space=pltpu.VMEM)
    hbm = pl.BlockSpec(memory_space=pl.ANY)
    slots = (REGIONS, CAP, WIDTH)
    scratch = [
        pltpu.VMEM((WIDTH, 3 * WIDTH), BF),
        pltpu.VMEM((WIDTH, WIDTH), BF),
        pltpu.SemaphoreType.DMA((2,)),
        *[pltpu.VMEM(slots, BF) for _ in range(8)],
        pltpu.VMEM((GROUPS, 8, 128), F32),
        pltpu.VMEM((REGIONS, 8, 128), F32),
        pltpu.VMEM((GROUPS, 8, 128), F32),
        pltpu.VMEM((REGIONS, 8, 128), F32),
        pltpu.VMEM((PTS, WIDTH), BF),
        pltpu.VMEM((WIDTH, PTS), BF),
        pltpu.VMEM((PTS, WIDTH), BF),
        pltpu.VMEM((PTS, PTS), F32),
        pltpu.VMEM((PTS, WIDTH), F32),
        pltpu.VMEM((PTS, WIDTH), BF),
        pltpu.VMEM((PTS, 3 * WIDTH), BF),
        pltpu.VMEM((PTS, WIDTH), BF),
        pltpu.VMEM((WIDTH, PTS), BF),
        pltpu.VMEM((WIDTH, PTS), BF),
        pltpu.VMEM((32, PTS, PTS), F32),
        pltpu.VMEM((WIDTH, PTS), BF),
        pltpu.VMEM((PTS, WIDTH), BF),
        pltpu.VMEM((WIDTH, PTS), BF),
        pltpu.VMEM((PTS, WIDTH), BF),
        pltpu.VMEM((PTS, 8 * PTS), BF),
        pltpu.VMEM((PTS, 8 * PTS), BF),
        pltpu.VMEM((8 * PTS, 128), BF),
        pltpu.VMEM((8 * PTS, 128), BF),
        pltpu.VMEM((PTS, 3 * WIDTH), BF),
        pltpu.VMEM((3 * WIDTH, PTS), BF),
        pltpu.VMEM((2, 4, 1024, 128), F32),
        pltpu.VMEM((4, 1024, 128), BF),
        pltpu.VMEM((4, 1024, 128), BF),
        pltpu.VMEM((4, 1024, 128), BF),
        pltpu.VMEM((4, 1024, 128), BF),
        pltpu.VMEM((REGIONS, 32, 128), BF),
        pltpu.VMEM((REGIONS, 32, 128), BF),
        pltpu.VMEM((4, 32, 128), F32),
        pltpu.VMEM((128, 128), F32),
        pltpu.SemaphoreType.DMA((12,)),
        pltpu.SemaphoreType.DMA((12,)),
    ]
    output, grad_points, grad_qkv, grad_proj, grad_gain, grad_bias = pl.pallas_call(
        kernel,
        out_shape=[
            jax.ShapeDtypeStruct((PTS, WIDTH), BF),
            jax.ShapeDtypeStruct((PTS, WIDTH), BF),
            jax.ShapeDtypeStruct((64, 48), F32),
            jax.ShapeDtypeStruct((64, 16), F32),
            jax.ShapeDtypeStruct((1, WIDTH), F32),
            jax.ShapeDtypeStruct((1, WIDTH), F32),
        ],
        in_specs=[vmem] * 6 + [hbm, hbm, vmem],
        out_specs=[vmem] * 6,
        scratch_shapes=scratch,
        compiler_params=pltpu.CompilerParams(
            collective_id=0, has_side_effects=True, vmem_limit_bytes=52 * 1024 * 1024
        ),
    )(
        points[0], row_slot, pos_slot, patch_ids[0], bn_gain[None], bn_bias[None],
        w_qkv, w_proj, cotangent[0],
    )
    return output[None], grad_points[None], grad_qkv, grad_proj, grad_gain[0], grad_bias[0]


def solution(mesh):
    placed = (
        P("group", "region", None),
        P("group", "region"),
        P("group", "region"),
        P("group", "region", None),
        P(),
        P(),
        P(),
        P(),
        P("group", "region", None),
    )
    return jax.shard_map(
        on_device,
        mesh=mesh,
        in_specs=placed,
        out_specs=(
            P("group", "region", None),
            P("group", "region", None),
            P("group", "region"),
            P("group", "region"),
            P(),
            P(),
        ),
        check_vma=False,
    )
```

```python
import functools

import jax
import jax.numpy as jnp
from jax import lax
from jax.experimental import pallas as pl
from jax.experimental.pallas import tpu as pltpu
from jax.sharding import PartitionSpec as P

HEAD_DIM = 16
EPS = 1e-05
PTS = 256
WIDTH = 512
CAP = 16
REGIONS = 32
GROUPS = 8
YS, ZS = 4, 8
CHUNK = 192
TOTAL = 65536
MESH = pl.DeviceIdType.MESH
BF = jnp.bfloat16
F32 = jnp.float32


def dot_nn(a, b):
    return jnp.dot(a, b, preferred_element_type=F32)


def dot_nt(a, b):
    return lax.dot_general(a, b, (((1,), (1,)), ((), ())), preferred_element_type=F32)


def as_column(row):
    return jnp.broadcast_to(row.astype(F32), (128, row.shape[1])).T.astype(jnp.int32)


def slot_rows(row):
    slots = lax.broadcasted_iota(jnp.int32, (REGIONS * CAP, PTS), 0)
    return jnp.where(slots == row, 1.0, 0.0).astype(BF)


def slot_columns(row):
    col = as_column(row)
    lane = lax.broadcasted_iota(jnp.int32, (PTS, 128), 1)
    parts = [jnp.where(col == lane + 128 * j, 1.0, 0.0) for j in range(4)]
    return jnp.concatenate(parts, axis=1).astype(BF)


def store_rows(ref, at, first, row):
    for j in range(4):
        ref[at, first + j : first + j + 1, :] = row[:, 128 * j : 128 * (j + 1)]


def load_row(block, first):
    return jnp.concatenate([block[first + j : first + j + 1, :] for j in range(4)], axis=1)


def kernel(
    x_hbm, rs_hbm, ps_hbm, pid_hbm, gain_hbm, bias_hbm, wqkv_hbm, wproj_hbm, cot_hbm,
    out_ref, gp_ref, gwq_ref, gwp_ref, gg_ref, gb_ref,
    x_ref, rs_ref, ps_ref, pid_ref, gain_ref, bias_ref, wqkv, wproj, cot_ref, in_sems,
    send_a, recv_a, send_b, recv_b, send_c, recv_c, send_d, recv_d,
    st1, st2, st3, gs1, gs2, gs3,
    p_t, q_n, q_t, aug_k, query_x, grad_x,
    unit_s, serial, qkv, qs, kt, value_x, es, heads, mixed_f, mixed_t, mixed,
    g_serial_t, gm, big_d, stack_g, stack_q, gqkv, left,
    g32, g_core, r_core, s_x, r_x, acc, s_y, r_y, s_z, r_z, fin,
    send_sems, recv_sems, core_send, core_recv, x_send, x_recv,
):
    r = lax.axis_index("region")
    g = lax.axis_index("group")
    xx, core = g // 2, g % 2
    yy, zz = r // ZS, r % ZS

    def each_region(act):
        def body(k, carry):
            act(lax.rem(r + k, REGIONS))
            return carry

        lax.fori_loop(1, REGIONS, body, 0)

    def each_group(act):
        def body(k, carry):
            act(lax.rem(g + k, GROUPS))
            return carry

        lax.fori_loop(1, GROUPS, body, 0)

    def remote(src, dst, send_sem, recv_sem, to):
        pltpu.make_async_remote_copy(
            src_ref=src, dst_ref=dst, send_sem=send_sem, recv_sem=recv_sem,
            device_id=to, device_id_type=MESH,
        ).start()

    def send(src, dst, stage, to):
        remote(src, dst, send_sems.at[stage], recv_sems.at[stage], to)

    def wait(ref, sem):
        pltpu.make_async_copy(ref, ref, sem).wait()

    def along_y(buf, stage):
        for k in range(1, YS):
            yp = lax.rem(yy + k, YS)
            send(buf.at[yy], buf.at[yy], stage, (yp * ZS + zz, g))

    def along_z(buf, stage):
        for k in range(1, ZS):
            zp = lax.rem(zz + k, ZS)
            send(buf.at[zz], buf.at[zz], stage, (yy * ZS + zp, g))

    def others(buf):
        return buf.at[pl.ds(0, buf.shape[0] - 1)]

    barrier = pltpu.get_barrier_semaphore()
    each_region(
        lambda p: pl.semaphore_signal(barrier, inc=1, device_id=(p, g), device_id_type=MESH)
    )
    each_group(
        lambda p: pl.semaphore_signal(barrier, inc=1, device_id=(r, p), device_id_type=MESH)
    )
    loads = [
        pltpu.make_async_copy(src, dst, in_sems.at[i])
        for i, (src, dst) in enumerate(
            [
                (rs_hbm, rs_ref), (x_hbm, x_ref), (ps_hbm, ps_ref), (pid_hbm, pid_ref),
                (cot_hbm, cot_ref), (gain_hbm, gain_ref), (bias_hbm, bias_ref),
                (wqkv_hbm, wqkv), (wproj_hbm, wproj),
            ]
        )
    ]
    for load in loads:
        load.start()

    loads[0].wait()
    p_n = slot_rows(rs_ref[...])
    loads[1].wait()
    x = x_ref[...]
    send_a[...] = dot_nn(p_n, x).astype(BF).reshape(REGIONS, CAP, WIDTH)

    pl.semaphore_wait(barrier, REGIONS - 1 + GROUPS - 1)

    each_region(lambda p: send(send_a.at[p], recv_a.at[r], 1, (p, g)))
    recv_a[r] = send_a[r]

    xf = x.astype(F32)
    mean_l = jnp.sum(xf, axis=0, keepdims=True) * (1.0 / PTS)
    dev = xf - mean_l
    store_rows(st1, g, 0, mean_l)
    store_rows(st1, g, 4, jnp.sum(dev * dev, axis=0, keepdims=True))
    each_group(lambda p: send(st1.at[g], st1.at[g], 0, (r, p)))

    for load in loads[2:]:
        load.wait()
    p_t[...] = slot_columns(rs_ref[...])
    q_n[...] = slot_rows(ps_ref[...])
    q_t[...] = slot_columns(ps_ref[...])
    send_b[...] = dot_nn(p_n, cot_ref[...]).astype(BF).reshape(REGIONS, CAP, WIDTH)
    pid_row = pid_ref[...]
    lane = lax.broadcasted_iota(jnp.int32, (PTS, 128), 1)
    aug_k[...] = jnp.where(
        (lane < 4) & (as_column(pid_row) != lane), -1e30, 0.0
    ).astype(BF)
    row = lax.broadcasted_iota(jnp.int32, (128, PTS), 0)
    same = jnp.where(row == pid_row, 1.0, 0.0).astype(BF)
    for j in range(4):
        query_x[j, 128:256, :] = same

    def merge(block, count, each):
        means, squares = block[:, 0:4, :], block[:, 4:8, :]
        mean = jnp.sum(means, axis=0) * (1.0 / count)
        off = means - mean[None]
        return mean, jnp.sum(squares, axis=0) + each * jnp.sum(off * off, axis=0)

    wait(others(st1), recv_sems.at[0])
    st2[yy, 0:4, :], st2[yy, 4:8, :] = merge(st1[...], GROUPS, float(PTS))
    along_y(st2, 2)
    wait(others(st2), recv_sems.at[2])
    st3[zz, 0:4, :], st3[zz, 4:8, :] = merge(st2[...], YS, float(PTS * GROUPS))
    along_z(st3, 9)

    each_region(lambda p: send(send_b.at[p], recv_b.at[r], 3, (p, g)))
    recv_b[r] = send_b[r]

    wait(others(st3), recv_sems.at[9])
    mean_4, square_4 = merge(st3[...], ZS, float(PTS * GROUPS * YS))
    inv_4 = lax.rsqrt(square_4 * (1.0 / TOTAL) + EPS)
    mean_all = load_row(mean_4, 0)
    inv_std = load_row(inv_4, 0)
    gain = gain_ref[...]

    wait(others(recv_a), recv_sems.at[1])
    pts = dot_nn(q_t[...], recv_a[...].reshape(REGIONS * CAP, WIDTH))
    unit = (pts - mean_all) * inv_std
    unit_s[...] = unit
    serial[...] = (unit * gain + bias_ref[...]).astype(BF)

    qkv[...] = dot_nn(serial[...], wqkv[...]).astype(BF)
    qs[...] = qkv[:, 0:WIDTH] * jnp.asarray(0.25, BF)
    kt[...] = qkv[:, WIDTH : 2 * WIDTH].T
    query_x[:, 0:128, :] = qs[...].T.reshape(4, 128, PTS)
    value_x[:, 0:HEAD_DIM, :] = qkv[:, 2 * WIDTH : 3 * WIDTH].T.reshape(32, HEAD_DIM, PTS)
    value_x[:, HEAD_DIM : 2 * HEAD_DIM, :] = jnp.ones((32, HEAD_DIM, PTS), BF)

    lane_1 = lax.broadcasted_iota(jnp.int32, (1, 128), 1)

    def head_mask(h):
        return jnp.where(lane_1 // HEAD_DIM == h, 1.0, 0.0).astype(BF)

    def forward(chunk, carry):
        col = pl.multiple_of(chunk * 128, 128)
        keys = qkv[:, pl.ds(WIDTH + col, 128)]
        for h in range(8):
            lhs = jnp.concatenate([keys * head_mask(h), aug_k[...]], axis=1)
            scores = dot_nn(lhs, query_x[chunk])
            e = jnp.exp(scores - jnp.max(scores, axis=0, keepdims=True)).astype(BF)
            es[chunk, :, PTS * h : PTS * (h + 1)] = e
            heads[chunk * 8 + h] = dot_nn(value_x[chunk * 8 + h], e)
        return carry

    lax.fori_loop(0, 4, forward, 0)
    inv_sum = 1.0 / heads[:, HEAD_DIM : HEAD_DIM + 1, :]
    mixed_f[...] = heads[:, 0:HEAD_DIM, :] * inv_sum
    mixed_t[...] = mixed_f[...].reshape(WIDTH, PTS).astype(BF)
    mixed[...] = mixed_t[...].T
    branch = dot_nn(mixed[...], wproj[...]).astype(BF)
    send_c[...] = dot_nn(q_n[...], branch).astype(BF).reshape(REGIONS, CAP, WIDTH)
    each_region(lambda p: send(send_c.at[p], recv_c.at[r], 4, (p, g)))
    recv_c[r] = send_c[r]

    sibling = (r, xx * 2 + 1 - core)

    def to_sibling(at, rows, slot):
        span = pl.ds(at, rows)
        g_core[span, :] = g32[1 - core, span, :].astype(BF)
        remote(g_core.at[span], r_core.at[span], core_send.at[slot], core_recv.at[slot], sibling)

    def to_chips(at, rows, slot):
        span = pl.ds(at, rows)
        wait(r_core.at[span], core_recv.at[slot])
        both = g32[core, span, :] + r_core[span, :].astype(F32)
        for b in range(4):
            s_x[b, span, :] = both[:, 128 * b : 128 * (b + 1)].astype(BF)
        for k in range(1, 4):
            xp = lax.rem(xx + k, 4)
            remote(
                s_x.at[xp, span], r_x.at[xx, span], x_send.at[slot], x_recv.at[slot],
                (r, xp * 2 + core),
            )

    wait(others(recv_b), recv_sems.at[3])
    g_serial = dot_nn(q_t[...], recv_b[...].reshape(REGIONS * CAP, WIDTH)).astype(BF)
    g_serial_t[...] = g_serial.T
    for part in range(4):
        rows = dot_nn(g_serial_t[128 * part : 128 * (part + 1), :], mixed[...])
        for u in range(8):
            at = 4 * CHUNK + part * 64 + (u // 2) * 16
            g32[(u + 1) % 2, at : at + 16, :] = rows[16 * u : 16 * (u + 1), :]
    to_sibling(4 * CHUNK, 256, 4)

    scaled = (
        dot_nn(wproj[...], g_serial_t[...]).reshape(32, HEAD_DIM, PTS) * inv_sum
    ).astype(BF)
    grad_x[:, 0:128, :] = scaled.reshape(4, 128, PTS)
    gm[...] = scaled.reshape(WIDTH, PTS).T
    inner = -jnp.sum(scaled.astype(F32) * mixed_f[...], axis=1, keepdims=True)
    first = inner.astype(BF).astype(F32)
    second = (inner - first).astype(BF).astype(F32)
    third = inner - first - second
    place = lax.broadcasted_iota(jnp.int32, (32, HEAD_DIM, PTS), 1)
    terms = jnp.where(
        place == 0, first, jnp.where(place == 1, second, jnp.where(place == 2, third, 0.0))
    )
    grad_x[:, 128:256, :] = terms.astype(BF).reshape(4, 128, PTS)

    def backward(chunk, carry):
        col = pl.multiple_of(chunk * 128, 128)
        values = qkv[:, pl.ds(2 * WIDTH + col, 128)]
        grads = gm[:, pl.ds(col, 128)]
        queries = qs[:, pl.ds(col, 128)]
        for h in range(8):
            mask = head_mask(h)
            span = slice(PTS * h, PTS * (h + 1))
            chosen = jnp.where(
                (lane_1 // HEAD_DIM == h) & (lane_1 % HEAD_DIM < 3), 1.0, 0.0
            ).astype(BF)
            lhs = jnp.concatenate(
                [values * mask, jnp.broadcast_to(chosen, (PTS, 128))], axis=1
            )
            ds = dot_nn(lhs, grad_x[chunk]).astype(BF) * es[chunk, :, span]
            big_d[:, span] = ds
            stack_g[span, :] = grads * mask
            stack_q[span, :] = queries * mask
            rows = pl.ds(pl.multiple_of(col + HEAD_DIM * h, HEAD_DIM), HEAD_DIM)
            left[HEAD_DIM * h : HEAD_DIM * (h + 1), :] = (dot_nn(kt[rows, :], ds) * 0.25).astype(BF)
        gqkv[:, pl.ds(col, 128)] = left[0:128, :].T
        gk = dot_nn(big_d[...], stack_q[...]).astype(BF)
        gqkv[:, pl.ds(WIDTH + col, 128)] = gk
        left[128:256, :] = gk.T
        gv = dot_nn(es[chunk], stack_g[...]).astype(BF)
        gqkv[:, pl.ds(2 * WIDTH + col, 128)] = gv
        left[256:384, :] = gv.T
        rows = dot_nn(left[...], serial[...])
        base = pl.multiple_of(chunk * CHUNK, 64)
        for p in range(3):
            for u in range(8):
                at = base + p * 64 + (u // 2) * 16
                g32[u % 2, pl.ds(at, 16), :] = rows[128 * p + 16 * u : 128 * p + 16 * (u + 1), :]
        to_sibling(base, CHUNK, chunk)

        @pl.when(chunk == 0)
        def _():
            to_chips(4 * CHUNK, 256, 4)

        @pl.when(chunk > 0)
        def _():
            to_chips(pl.multiple_of((chunk - 1) * CHUNK, 64), CHUNK, chunk - 1)

        return carry

    lax.fori_loop(0, 4, backward, 0)

    grad_in = dot_nt(gqkv[...], wqkv[...]).astype(BF)
    send_d[...] = dot_nn(q_n[...], grad_in).astype(BF).reshape(REGIONS, CAP, WIDTH)
    each_region(lambda p: send(send_d.at[p], recv_d.at[r], 7, (p, g)))
    recv_d[r] = send_d[r]
    to_chips(3 * CHUNK, CHUNK, 3)
    grad_f = grad_in.astype(F32)
    store_rows(gs1, g, 0, jnp.sum(grad_f, axis=0, keepdims=True))
    store_rows(gs1, g, 4, jnp.sum(grad_f * unit_s[...], axis=0, keepdims=True))
    each_group(lambda p: send(gs1.at[g], gs1.at[g], 6, (r, p)))

    wait(others(recv_c), recv_sems.at[4])
    out_ref[...] = dot_nn(p_t[...], recv_c[...].reshape(REGIONS * CAP, WIDTH)).astype(BF)

    wait(others(gs1), recv_sems.at[6])
    gs2[yy] = jnp.sum(gs1[...], axis=0)
    along_y(gs2, 8)

    def gather_chunk(at, rows, slot):
        wait(r_x.at[pl.ds(0, 3), pl.ds(at, rows)], x_recv.at[slot])
        span = slice(at, at + rows)
        mine = pl.ds(pl.multiple_of(xx * 128, 128), 128)
        total = g32[core, span, mine] + r_core[span, mine].astype(F32)
        for k in range(1, 4):
            total = total + r_x[lax.rem(xx + k, 4), span, :].astype(F32)
        return total.astype(BF)

    acc[768:1024, :] = gather_chunk(4 * CHUNK, 256, 4)
    for j in range(4):
        total = gather_chunk(j * CHUNK, CHUNK, j)
        for p in range(3):
            acc[256 * p + 64 * j : 256 * p + 64 * (j + 1), :] = total[64 * p : 64 * (p + 1), :]

    def unit_rows(at):
        return acc[pl.ds(pl.multiple_of(at * 16, 16), 16), :]

    for i in range(16):
        a, b = 2 * i + core, 2 * i + 1 - core
        s_y[a, 0:16, :] = unit_rows(3 * i + core)
        s_y[a, 16:32, :] = unit_rows(3 * i + core + 1)
        s_y[b, 0:16, :] = unit_rows(3 * i + 2 - 2 * core)
        s_y[b, 16:32, :] = unit_rows(48 + i)

    def y_part(at):
        return pl.ds(pl.multiple_of(at * ZS, ZS), ZS)

    for k in range(1, YS):
        yp = lax.rem(yy + k, YS)
        send(s_y.at[y_part(yp)], r_y.at[y_part(yy)], 10, (yp * ZS + zz, g))
    r_y[y_part(yy)] = s_y[y_part(yy)]

    wait(others(gs2), recv_sems.at[8])
    gs3[zz] = jnp.sum(gs2[...], axis=0)
    along_z(gs3, 5)

    wait(r_y.at[pl.ds(0, 3 * ZS)], recv_sems.at[10])
    s_z[...] = jnp.sum(r_y[...].astype(F32).reshape(YS, ZS, 32, 128), axis=0).astype(BF)
    for k in range(1, ZS):
        zp = lax.rem(zz + k, ZS)
        send(s_z.at[zp], r_z.at[zz], 12, (yy * ZS + zp, g))
    r_z[zz] = s_z[zz]

    wait(others(gs3), recv_sems.at[5])
    sums = jnp.sum(gs3[...], axis=0)
    grad_bias = load_row(sums, 0)
    grad_gain = load_row(sums, 4)
    gb_ref[...] = grad_bias
    gg_ref[...] = grad_gain

    wait(others(r_z), recv_sems.at[12])
    fin[core] = jnp.sum(r_z[...].astype(F32), axis=0)
    send(fin.at[core], fin.at[core], 11, sibling)

    wait(others(recv_d), recv_sems.at[7])
    grad_n = dot_nn(p_t[...], recv_d[...].reshape(REGIONS * CAP, WIDTH))
    unit_b = (x_ref[...].astype(F32) - mean_all) * inv_std
    scale = 1.0 / TOTAL
    gp_ref[...] = (
        inv_std
        * (grad_n * gain - gain * grad_bias * scale - unit_b * (gain * grad_gain * scale))
    ).astype(BF)

    wait(fin.at[0], recv_sems.at[11])
    even, odd = fin[r % 2], fin[1 - r % 2]

    def my_lanes(rows):
        return jnp.where(core == 0, rows[:, 0:64], rows[:, 64:128])

    gwq_ref[0:16, :] = my_lanes(even[0:16, :])
    gwq_ref[16:32, :] = my_lanes(odd[0:16, :])
    gwq_ref[32:48, :] = my_lanes(even[16:32, :])
    gwp_ref[...] = my_lanes(odd[16:32, :])

    for buf, stage in (
        (st1, 0), (send_a, 1), (st2, 2), (send_b, 3), (send_c, 4), (gs3, 5), (gs1, 6),
        (send_d, 7), (gs2, 8), (st3, 9), (r_z, 12),
    ):
        wait(others(buf), send_sems.at[stage])
    wait(s_y.at[pl.ds(0, 3 * ZS)], send_sems.at[10])
    wait(fin.at[0], send_sems.at[11])
    for slot, at, rows in [(j, j * CHUNK, CHUNK) for j in range(4)] + [(4, 4 * CHUNK, 256)]:
        wait(g_core.at[pl.ds(at, rows)], core_send.at[slot])
        wait(s_x.at[pl.ds(0, 3), pl.ds(at, rows)], x_send.at[slot])


def deliver(*refs):
    n = len(refs) // 2
    sems = refs[-1]
    copies = [pltpu.make_async_copy(refs[i], refs[n + i], sems.at[i]) for i in range(n)]
    for copy in copies:
        copy.start()
    for copy in copies:
        copy.wait()


def on_device(points, row_slot, pos_slot, patch_ids, bn_gain, bn_bias, w_qkv, w_proj, cotangent):
    vmem = pl.BlockSpec(memory_space=pltpu.VMEM)
    hbm = pl.BlockSpec(memory_space=pltpu.HBM)
    args = tuple(pltpu.with_memory_space_constraint(a, pltpu.HBM) for a in (
        points[0], row_slot, pos_slot, patch_ids[0], bn_gain[None], bn_bias[None],
        w_qkv, w_proj, cotangent[0],
    ))

    def buf(dtype, *shape):
        return pltpu.VMEM(shape, dtype)

    scratch = [buf(a.dtype, *a.shape) for a in args]
    scratch += [pltpu.SemaphoreType.DMA((9,))]
    scratch += [buf(BF, REGIONS, CAP, WIDTH) for _ in range(8)]
    scratch += [buf(F32, n, 8, 128) for n in (GROUPS, YS, ZS, GROUPS, YS, ZS)]
    scratch += [
        buf(BF, PTS, WIDTH),
        buf(BF, WIDTH, PTS),
        buf(BF, PTS, WIDTH),
        buf(BF, PTS, 128),
        buf(BF, 4, 256, PTS),
        buf(BF, 4, 256, PTS),
        buf(F32, PTS, WIDTH),
        buf(BF, PTS, WIDTH),
        buf(BF, PTS, 3 * WIDTH),
        buf(BF, PTS, WIDTH),
        buf(BF, WIDTH, PTS),
        buf(BF, 32, 2 * HEAD_DIM, PTS),
        buf(BF, 4, PTS, 8 * PTS),
        buf(F32, 32, 2 * HEAD_DIM, PTS),
        buf(F32, 32, HEAD_DIM, PTS),
        buf(BF, WIDTH, PTS),
        buf(BF, PTS, WIDTH),
        buf(BF, WIDTH, PTS),
        buf(BF, PTS, WIDTH),
        buf(BF, PTS, 8 * PTS),
        buf(BF, 8 * PTS, 128),
        buf(BF, 8 * PTS, 128),
        buf(BF, PTS, 3 * WIDTH),
        buf(BF, 384, PTS),
        buf(F32, 2, 1024, WIDTH),
        buf(BF, 1024, WIDTH),
        buf(BF, 1024, WIDTH),
        buf(BF, 4, 1024, 128),
        buf(BF, 4, 1024, 128),
        buf(BF, 1024, 128),
        buf(BF, REGIONS, 32, 128),
        buf(BF, REGIONS, 32, 128),
        buf(BF, ZS, 32, 128),
        buf(BF, ZS, 32, 128),
        buf(F32, 2, 32, 128),
    ]
    scratch += [pltpu.SemaphoreType.DMA((n,)) for n in (13, 13, 5, 5, 5, 5)]
    shapes = [
        jax.ShapeDtypeStruct((PTS, WIDTH), BF),
        jax.ShapeDtypeStruct((PTS, WIDTH), BF),
        jax.ShapeDtypeStruct((48, 64), F32),
        jax.ShapeDtypeStruct((16, 64), F32),
        jax.ShapeDtypeStruct((1, WIDTH), F32),
        jax.ShapeDtypeStruct((1, WIDTH), F32),
    ]
    results = pl.pallas_call(
        kernel,
        out_shape=shapes,
        in_specs=[hbm] * 9,
        out_specs=[vmem] * 6,
        scratch_shapes=scratch,
        compiler_params=pltpu.CompilerParams(
            collective_id=0, has_side_effects=True, vmem_limit_bytes=52 * 1024 * 1024
        ),
    )(*args)
    output, grad_points, grad_qkv, grad_proj, grad_gain, grad_bias = pl.pallas_call(
        deliver,
        out_shape=shapes,
        in_specs=[vmem] * 6,
        out_specs=[hbm] * 6,
        scratch_shapes=[pltpu.SemaphoreType.DMA((6,))],
    )(*results)
    return output[None], grad_points[None], grad_qkv.T, grad_proj.T, grad_gain[0], grad_bias[0]


def solution(mesh):
    placed = (
        P("group", "region", None),
        P("group", "region"),
        P("group", "region"),
        P("group", "region", None),
        P(),
        P(),
        P(),
        P(),
        P("group", "region", None),
    )
    return jax.shard_map(
        on_device,
        mesh=mesh,
        in_specs=placed,
        out_specs=(
            P("group", "region", None),
            P("group", "region", None),
            P("group", "region"),
            P("group", "region"),
            P(),
            P(),
        ),
        check_vma=False,
    )
```

```python
import functools

import jax
import jax.numpy as jnp
from jax import lax
from jax.experimental import pallas as pl
from jax.experimental.pallas import tpu as pltpu
from jax.sharding import PartitionSpec as P

HEAD_DIM = 16
EPS = 1e-05
PTS = 256
WIDTH = 512
CAP = 16
REGIONS = 32
GROUPS = 8
YS, ZS = 4, 8
CHUNK = 192
TOTAL = 65536
MESH = pl.DeviceIdType.MESH
BF = jnp.bfloat16
F32 = jnp.float32


def dot_nn(a, b):
    return jnp.dot(a, b, preferred_element_type=F32)


def dot_nt(a, b):
    return lax.dot_general(a, b, (((1,), (1,)), ((), ())), preferred_element_type=F32)


def as_column(row):
    return jnp.broadcast_to(row.astype(F32), (128, row.shape[1])).T.astype(jnp.int32)


def slot_rows(row):
    slots = lax.broadcasted_iota(jnp.int32, (REGIONS * CAP, PTS), 0)
    return jnp.where(slots == row, 1.0, 0.0).astype(BF)


def slot_columns(row):
    col = as_column(row)
    lane = lax.broadcasted_iota(jnp.int32, (PTS, 128), 1)
    parts = [jnp.where(col == lane + 128 * j, 1.0, 0.0) for j in range(4)]
    return jnp.concatenate(parts, axis=1).astype(BF)


def store_rows(ref, at, first, row):
    for j in range(4):
        ref[at, first + j : first + j + 1, :] = row[:, 128 * j : 128 * (j + 1)]


def load_row(block, first):
    return jnp.concatenate([block[first + j : first + j + 1, :] for j in range(4)], axis=1)


def kernel(
    x_hbm, rs_hbm, ps_hbm, pid_hbm, gain_hbm, bias_hbm, wqkv_hbm, wproj_hbm, cot_hbm,
    out_ref, gp_ref, gwq_ref, gwp_ref, gg_ref, gb_ref,
    x_ref, rs_ref, ps_ref, pid_ref, gain_ref, bias_ref, wqkv, wproj, cot_ref, in_sems,
    send_a, recv_a, send_b, recv_b, send_c, recv_c, send_d, recv_d,
    st1, st2, st3, gs1, gs2, gs3,
    p_t, q_n, q_t, aug_k, query_x, grad_x,
    unit_s, serial, qkv, qs, kt, value_x, score, es, heads, mixed_f, mixed_t, mixed,
    g_serial_t, gm, big_d, stack_g, stack_q, gqkv, left,
    g32, g_core, r_core, s_x, r_x, acc, s_y, r_y, s_z, r_z, fin,
    send_sems, recv_sems, core_send, core_recv, x_send, x_recv,
):
    r = lax.axis_index("region")
    g = lax.axis_index("group")
    xx, core = g // 2, g % 2
    yy, zz = r // ZS, r % ZS

    def each_region(act):
        def body(k, carry):
            act(lax.rem(r + k, REGIONS))
            return carry

        lax.fori_loop(1, REGIONS, body, 0)

    def each_group(act):
        def body(k, carry):
            act(lax.rem(g + k, GROUPS))
            return carry

        lax.fori_loop(1, GROUPS, body, 0)

    def remote(src, dst, send_sem, recv_sem, to):
        pltpu.make_async_remote_copy(
            src_ref=src, dst_ref=dst, send_sem=send_sem, recv_sem=recv_sem,
            device_id=to, device_id_type=MESH,
        ).start()

    def send(src, dst, stage, to):
        remote(src, dst, send_sems.at[stage], recv_sems.at[stage], to)

    def wait(ref, sem):
        pltpu.make_async_copy(ref, ref, sem).wait()

    def along_y(buf, stage):
        for k in range(1, YS):
            yp = lax.rem(yy + k, YS)
            send(buf.at[yy], buf.at[yy], stage, (yp * ZS + zz, g))

    def along_z(buf, stage):
        for k in range(1, ZS):
            zp = lax.rem(zz + k, ZS)
            send(buf.at[zz], buf.at[zz], stage, (yy * ZS + zp, g))

    def others(buf):
        return buf.at[pl.ds(0, buf.shape[0] - 1)]

    barrier = pltpu.get_barrier_semaphore()
    each_region(
        lambda p: pl.semaphore_signal(barrier, inc=1, device_id=(p, g), device_id_type=MESH)
    )
    each_group(
        lambda p: pl.semaphore_signal(barrier, inc=1, device_id=(r, p), device_id_type=MESH)
    )
    loads = [
        pltpu.make_async_copy(src, dst, in_sems.at[i])
        for i, (src, dst) in enumerate(
            [
                (rs_hbm, rs_ref), (x_hbm, x_ref), (ps_hbm, ps_ref), (pid_hbm, pid_ref),
                (cot_hbm, cot_ref), (gain_hbm, gain_ref), (bias_hbm, bias_ref),
                (wqkv_hbm, wqkv), (wproj_hbm, wproj),
            ]
        )
    ]
    for load in loads:
        load.start()

    loads[0].wait()
    p_n = slot_rows(rs_ref[...])
    loads[1].wait()
    x = x_ref[...]
    send_a[...] = dot_nn(p_n, x).astype(BF).reshape(REGIONS, CAP, WIDTH)

    pl.semaphore_wait(barrier, REGIONS - 1 + GROUPS - 1)

    each_region(lambda p: send(send_a.at[p], recv_a.at[r], 1, (p, g)))
    recv_a[r] = send_a[r]

    xf = x.astype(F32)
    mean_l = jnp.sum(xf, axis=0, keepdims=True) * (1.0 / PTS)
    dev = xf - mean_l
    store_rows(st1, g, 0, mean_l)
    store_rows(st1, g, 4, jnp.sum(dev * dev, axis=0, keepdims=True))
    each_group(lambda p: send(st1.at[g], st1.at[g], 0, (r, p)))

    for load in loads[2:]:
        load.wait()
    p_t[...] = slot_columns(rs_ref[...])
    q_n[...] = slot_rows(ps_ref[...])
    q_t[...] = slot_columns(ps_ref[...])
    send_b[...] = dot_nn(p_n, cot_ref[...]).astype(BF).reshape(REGIONS, CAP, WIDTH)
    pid_row = pid_ref[...]
    lane = lax.broadcasted_iota(jnp.int32, (PTS, 128), 1)
    aug_k[...] = jnp.where(
        (lane < 4) & (as_column(pid_row) != lane), -1e30, 0.0
    ).astype(BF)
    row = lax.broadcasted_iota(jnp.int32, (128, PTS), 0)
    same = jnp.where(row == pid_row, 1.0, 0.0).astype(BF)
    for j in range(4):
        query_x[j, 128:256, :] = same

    def merge(block, count, each):
        means, squares = block[:, 0:4, :], block[:, 4:8, :]
        mean = jnp.sum(means, axis=0) * (1.0 / count)
        off = means - mean[None]
        return mean, jnp.sum(squares, axis=0) + each * jnp.sum(off * off, axis=0)

    wait(others(st1), recv_sems.at[0])
    st2[yy, 0:4, :], st2[yy, 4:8, :] = merge(st1[...], GROUPS, float(PTS))
    along_y(st2, 2)
    wait(others(st2), recv_sems.at[2])
    st3[zz, 0:4, :], st3[zz, 4:8, :] = merge(st2[...], YS, float(PTS * GROUPS))
    along_z(st3, 9)

    each_region(lambda p: send(send_b.at[p], recv_b.at[r], 3, (p, g)))
    recv_b[r] = send_b[r]

    wait(others(st3), recv_sems.at[9])
    mean_4, square_4 = merge(st3[...], ZS, float(PTS * GROUPS * YS))
    inv_4 = lax.rsqrt(square_4 * (1.0 / TOTAL) + EPS)
    mean_all = load_row(mean_4, 0)
    inv_std = load_row(inv_4, 0)
    gain = gain_ref[...]

    wait(others(recv_a), recv_sems.at[1])
    pts = dot_nn(q_t[...], recv_a[...].reshape(REGIONS * CAP, WIDTH))
    unit = (pts - mean_all) * inv_std
    unit_s[...] = unit
    serial[...] = (unit * gain + bias_ref[...]).astype(BF)

    qkv[...] = dot_nn(serial[...], wqkv[...]).astype(BF)
    qs[...] = qkv[:, 0:WIDTH] * jnp.asarray(0.25, BF)
    kt[...] = qkv[:, WIDTH : 2 * WIDTH].T
    query_x[:, 0:128, :] = qs[...].T.reshape(4, 128, PTS)
    value_x[:, 0:HEAD_DIM, :] = qkv[:, 2 * WIDTH : 3 * WIDTH].T.reshape(32, HEAD_DIM, PTS)
    value_x[:, HEAD_DIM : 2 * HEAD_DIM, :] = jnp.ones((32, HEAD_DIM, PTS), BF)

    lane_1 = lax.broadcasted_iota(jnp.int32, (1, 128), 1)

    def head_mask(h):
        return jnp.where(lane_1 // HEAD_DIM == h, 1.0, 0.0).astype(BF)

    def forward(chunk, carry):
        col = pl.multiple_of(chunk * 128, 128)
        keys = qkv[:, pl.ds(WIDTH + col, 128)]
        for h in range(8):
            lhs = jnp.concatenate([keys * head_mask(h), aug_k[...]], axis=1)
            score[h] = dot_nn(lhs, query_x[chunk])
        for h in range(8):
            top = jnp.max(score[h], axis=0, keepdims=True)
            es[chunk, :, PTS * h : PTS * (h + 1)] = jnp.exp(score[h] - top).astype(BF)
        for h in range(8):
            e = es[chunk, :, PTS * h : PTS * (h + 1)]
            heads[chunk * 8 + h] = dot_nn(value_x[chunk * 8 + h], e)
        return carry

    lax.fori_loop(0, 4, forward, 0)
    inv_sum = 1.0 / heads[:, HEAD_DIM : HEAD_DIM + 1, :]
    mixed_f[...] = heads[:, 0:HEAD_DIM, :] * inv_sum
    mixed_t[...] = mixed_f[...].reshape(WIDTH, PTS).astype(BF)
    mixed[...] = mixed_t[...].T
    branch = dot_nn(mixed[...], wproj[...]).astype(BF)
    send_c[...] = dot_nn(q_n[...], branch).astype(BF).reshape(REGIONS, CAP, WIDTH)
    each_region(lambda p: send(send_c.at[p], recv_c.at[r], 4, (p, g)))
    recv_c[r] = send_c[r]

    sibling = (r, xx * 2 + 1 - core)

    def to_sibling(at, rows, slot):
        span = pl.ds(at, rows)
        g_core[span, :] = g32[1 - core, span, :].astype(BF)
        remote(g_core.at[span], r_core.at[span], core_send.at[slot], core_recv.at[slot], sibling)

    def to_chips(at, rows, slot):
        span = pl.ds(at, rows)
        wait(r_core.at[span], core_recv.at[slot])
        both = g32[core, span, :] + r_core[span, :].astype(F32)
        for b in range(4):
            s_x[b, span, :] = both[:, 128 * b : 128 * (b + 1)].astype(BF)
        for k in range(1, 4):
            xp = lax.rem(xx + k, 4)
            remote(
                s_x.at[xp, span], r_x.at[xx, span], x_send.at[slot], x_recv.at[slot],
                (r, xp * 2 + core),
            )

    wait(others(recv_b), recv_sems.at[3])
    g_serial = dot_nn(q_t[...], recv_b[...].reshape(REGIONS * CAP, WIDTH)).astype(BF)
    g_serial_t[...] = g_serial.T
    for part in range(4):
        rows = dot_nn(g_serial_t[128 * part : 128 * (part + 1), :], mixed[...])
        for u in range(8):
            at = 4 * CHUNK + part * 64 + (u // 2) * 16
            g32[(u + 1) % 2, at : at + 16, :] = rows[16 * u : 16 * (u + 1), :]
    to_sibling(4 * CHUNK, 256, 4)

    scaled = (
        dot_nn(wproj[...], g_serial_t[...]).reshape(32, HEAD_DIM, PTS) * inv_sum
    ).astype(BF)
    grad_x[:, 0:128, :] = scaled.reshape(4, 128, PTS)
    gm[...] = scaled.reshape(WIDTH, PTS).T
    inner = -jnp.sum(scaled.astype(F32) * mixed_f[...], axis=1, keepdims=True)
    first = inner.astype(BF).astype(F32)
    second = (inner - first).astype(BF).astype(F32)
    third = inner - first - second
    place = lax.broadcasted_iota(jnp.int32, (32, HEAD_DIM, PTS), 1)
    terms = jnp.where(
        place == 0, first, jnp.where(place == 1, second, jnp.where(place == 2, third, 0.0))
    )
    grad_x[:, 128:256, :] = terms.astype(BF).reshape(4, 128, PTS)

    def backward(chunk, carry):
        col = pl.multiple_of(chunk * 128, 128)
        values = qkv[:, pl.ds(2 * WIDTH + col, 128)]
        grads = gm[:, pl.ds(col, 128)]
        queries = qs[:, pl.ds(col, 128)]
        spans = [slice(PTS * h, PTS * (h + 1)) for h in range(8)]
        for h in range(8):
            stack_g[spans[h], :] = grads * head_mask(h)
            stack_q[spans[h], :] = queries * head_mask(h)
        for h in range(8):
            chosen = jnp.where(
                (lane_1 // HEAD_DIM == h) & (lane_1 % HEAD_DIM < 3), 1.0, 0.0
            ).astype(BF)
            lhs = jnp.concatenate(
                [values * head_mask(h), jnp.broadcast_to(chosen, (PTS, 128))], axis=1
            )
            ds = dot_nn(lhs, grad_x[chunk]).astype(BF) * es[chunk, :, spans[h]]
            big_d[:, spans[h]] = ds
        for h in range(8):
            rows = pl.ds(pl.multiple_of(col + HEAD_DIM * h, HEAD_DIM), HEAD_DIM)
            left[HEAD_DIM * h : HEAD_DIM * (h + 1), :] = (
                dot_nn(kt[rows, :], big_d[:, spans[h]]) * 0.25
            ).astype(BF)
        gqkv[:, pl.ds(col, 128)] = left[0:128, :].T
        gk = dot_nn(big_d[...], stack_q[...]).astype(BF)
        gqkv[:, pl.ds(WIDTH + col, 128)] = gk
        left[128:256, :] = gk.T
        gv = dot_nn(es[chunk], stack_g[...]).astype(BF)
        gqkv[:, pl.ds(2 * WIDTH + col, 128)] = gv
        left[256:384, :] = gv.T
        rows = dot_nn(left[...], serial[...])
        base = pl.multiple_of(chunk * CHUNK, 64)
        for p in range(3):
            for u in range(8):
                at = base + p * 64 + (u // 2) * 16
                g32[u % 2, pl.ds(at, 16), :] = rows[128 * p + 16 * u : 128 * p + 16 * (u + 1), :]
        to_sibling(base, CHUNK, chunk)

        @pl.when(chunk == 0)
        def _():
            to_chips(4 * CHUNK, 256, 4)

        @pl.when(chunk > 0)
        def _():
            to_chips(pl.multiple_of((chunk - 1) * CHUNK, 64), CHUNK, chunk - 1)

        return carry

    lax.fori_loop(0, 4, backward, 0)

    grad_in = dot_nt(gqkv[...], wqkv[...]).astype(BF)
    send_d[...] = dot_nn(q_n[...], grad_in).astype(BF).reshape(REGIONS, CAP, WIDTH)
    each_region(lambda p: send(send_d.at[p], recv_d.at[r], 7, (p, g)))
    recv_d[r] = send_d[r]
    to_chips(3 * CHUNK, CHUNK, 3)
    grad_f = grad_in.astype(F32)
    store_rows(gs1, g, 0, jnp.sum(grad_f, axis=0, keepdims=True))
    store_rows(gs1, g, 4, jnp.sum(grad_f * unit_s[...], axis=0, keepdims=True))
    each_group(lambda p: send(gs1.at[g], gs1.at[g], 6, (r, p)))

    wait(others(recv_c), recv_sems.at[4])
    out_ref[...] = dot_nn(p_t[...], recv_c[...].reshape(REGIONS * CAP, WIDTH)).astype(BF)

    wait(others(gs1), recv_sems.at[6])
    gs2[yy] = jnp.sum(gs1[...], axis=0)
    along_y(gs2, 8)

    def gather_chunk(at, rows, slot):
        wait(r_x.at[pl.ds(0, 3), pl.ds(at, rows)], x_recv.at[slot])
        span = slice(at, at + rows)
        mine = pl.ds(pl.multiple_of(xx * 128, 128), 128)
        total = g32[core, span, mine] + r_core[span, mine].astype(F32)
        for k in range(1, 4):
            total = total + r_x[lax.rem(xx + k, 4), span, :].astype(F32)
        return total.astype(BF)

    acc[768:1024, :] = gather_chunk(4 * CHUNK, 256, 4)
    for j in range(4):
        total = gather_chunk(j * CHUNK, CHUNK, j)
        for p in range(3):
            acc[256 * p + 64 * j : 256 * p + 64 * (j + 1), :] = total[64 * p : 64 * (p + 1), :]

    def unit_rows(at):
        return acc[pl.ds(pl.multiple_of(at * 16, 16), 16), :]

    for i in range(16):
        a, b = 2 * i + core, 2 * i + 1 - core
        s_y[a, 0:16, :] = unit_rows(3 * i + core)
        s_y[a, 16:32, :] = unit_rows(3 * i + core + 1)
        s_y[b, 0:16, :] = unit_rows(3 * i + 2 - 2 * core)
        s_y[b, 16:32, :] = unit_rows(48 + i)

    def y_part(at):
        return pl.ds(pl.multiple_of(at * ZS, ZS), ZS)

    for k in range(1, YS):
        yp = lax.rem(yy + k, YS)
        send(s_y.at[y_part(yp)], r_y.at[y_part(yy)], 10, (yp * ZS + zz, g))
    r_y[y_part(yy)] = s_y[y_part(yy)]

    wait(others(gs2), recv_sems.at[8])
    gs3[zz] = jnp.sum(gs2[...], axis=0)
    along_z(gs3, 5)

    wait(r_y.at[pl.ds(0, 3 * ZS)], recv_sems.at[10])
    s_z[...] = jnp.sum(r_y[...].astype(F32).reshape(YS, ZS, 32, 128), axis=0).astype(BF)
    for k in range(1, ZS):
        zp = lax.rem(zz + k, ZS)
        send(s_z.at[zp], r_z.at[zz], 12, (yy * ZS + zp, g))
    r_z[zz] = s_z[zz]

    wait(others(gs3), recv_sems.at[5])
    sums = jnp.sum(gs3[...], axis=0)
    grad_bias = load_row(sums, 0)
    grad_gain = load_row(sums, 4)
    gb_ref[...] = grad_bias
    gg_ref[...] = grad_gain

    wait(others(r_z), recv_sems.at[12])
    fin[core] = jnp.sum(r_z[...].astype(F32), axis=0)
    send(fin.at[core], fin.at[core], 11, sibling)

    wait(others(recv_d), recv_sems.at[7])
    grad_n = dot_nn(p_t[...], recv_d[...].reshape(REGIONS * CAP, WIDTH))
    unit_b = (x_ref[...].astype(F32) - mean_all) * inv_std
    scale = 1.0 / TOTAL
    gp_ref[...] = (
        inv_std
        * (grad_n * gain - gain * grad_bias * scale - unit_b * (gain * grad_gain * scale))
    ).astype(BF)

    wait(fin.at[0], recv_sems.at[11])
    even, odd = fin[r % 2], fin[1 - r % 2]

    def my_lanes(rows):
        return jnp.where(core == 0, rows[:, 0:64], rows[:, 64:128])

    gwq_ref[0:16, :] = my_lanes(even[0:16, :])
    gwq_ref[16:32, :] = my_lanes(odd[0:16, :])
    gwq_ref[32:48, :] = my_lanes(even[16:32, :])
    gwp_ref[...] = my_lanes(odd[16:32, :])

    for buf, stage in (
        (st1, 0), (send_a, 1), (st2, 2), (send_b, 3), (send_c, 4), (gs3, 5), (gs1, 6),
        (send_d, 7), (gs2, 8), (st3, 9), (r_z, 12),
    ):
        wait(others(buf), send_sems.at[stage])
    wait(s_y.at[pl.ds(0, 3 * ZS)], send_sems.at[10])
    wait(fin.at[0], send_sems.at[11])
    for slot, at, rows in [(j, j * CHUNK, CHUNK) for j in range(4)] + [(4, 4 * CHUNK, 256)]:
        wait(g_core.at[pl.ds(at, rows)], core_send.at[slot])
        wait(s_x.at[pl.ds(0, 3), pl.ds(at, rows)], x_send.at[slot])


def deliver(*refs):
    n = len(refs) // 2
    sems = refs[-1]
    copies = [pltpu.make_async_copy(refs[i], refs[n + i], sems.at[i]) for i in range(n)]
    for copy in copies:
        copy.start()
    for copy in copies:
        copy.wait()


def on_device(points, row_slot, pos_slot, patch_ids, bn_gain, bn_bias, w_qkv, w_proj, cotangent):
    vmem = pl.BlockSpec(memory_space=pltpu.VMEM)
    hbm = pl.BlockSpec(memory_space=pltpu.HBM)
    args = tuple(pltpu.with_memory_space_constraint(a, pltpu.HBM) for a in (
        points[0], row_slot, pos_slot, patch_ids[0], bn_gain[None], bn_bias[None],
        w_qkv, w_proj, cotangent[0],
    ))

    def buf(dtype, *shape):
        return pltpu.VMEM(shape, dtype)

    scratch = [buf(a.dtype, *a.shape) for a in args]
    scratch += [pltpu.SemaphoreType.DMA((9,))]
    scratch += [buf(BF, REGIONS, CAP, WIDTH) for _ in range(8)]
    scratch += [buf(F32, n, 8, 128) for n in (GROUPS, YS, ZS, GROUPS, YS, ZS)]
    scratch += [
        buf(BF, PTS, WIDTH),
        buf(BF, WIDTH, PTS),
        buf(BF, PTS, WIDTH),
        buf(BF, PTS, 128),
        buf(BF, 4, 256, PTS),
        buf(BF, 4, 256, PTS),
        buf(F32, PTS, WIDTH),
        buf(BF, PTS, WIDTH),
        buf(BF, PTS, 3 * WIDTH),
        buf(BF, PTS, WIDTH),
        buf(BF, WIDTH, PTS),
        buf(BF, 32, 2 * HEAD_DIM, PTS),
        buf(F32, 8, PTS, PTS),
        buf(BF, 4, PTS, 8 * PTS),
        buf(F32, 32, 2 * HEAD_DIM, PTS),
        buf(F32, 32, HEAD_DIM, PTS),
        buf(BF, WIDTH, PTS),
        buf(BF, PTS, WIDTH),
        buf(BF, WIDTH, PTS),
        buf(BF, PTS, WIDTH),
        buf(BF, PTS, 8 * PTS),
        buf(BF, 8 * PTS, 128),
        buf(BF, 8 * PTS, 128),
        buf(BF, PTS, 3 * WIDTH),
        buf(BF, 384, PTS),
        buf(F32, 2, 1024, WIDTH),
        buf(BF, 1024, WIDTH),
        buf(BF, 1024, WIDTH),
        buf(BF, 4, 1024, 128),
        buf(BF, 4, 1024, 128),
        buf(BF, 1024, 128),
        buf(BF, REGIONS, 32, 128),
        buf(BF, REGIONS, 32, 128),
        buf(BF, ZS, 32, 128),
        buf(BF, ZS, 32, 128),
        buf(F32, 2, 32, 128),
    ]
    scratch += [pltpu.SemaphoreType.DMA((n,)) for n in (13, 13, 5, 5, 5, 5)]
    shapes = [
        jax.ShapeDtypeStruct((PTS, WIDTH), BF),
        jax.ShapeDtypeStruct((PTS, WIDTH), BF),
        jax.ShapeDtypeStruct((48, 64), F32),
        jax.ShapeDtypeStruct((16, 64), F32),
        jax.ShapeDtypeStruct((1, WIDTH), F32),
        jax.ShapeDtypeStruct((1, WIDTH), F32),
    ]
    results = pl.pallas_call(
        kernel,
        out_shape=shapes,
        in_specs=[hbm] * 9,
        out_specs=[vmem] * 6,
        scratch_shapes=scratch,
        compiler_params=pltpu.CompilerParams(
            collective_id=0, has_side_effects=True, vmem_limit_bytes=52 * 1024 * 1024
        ),
    )(*args)
    output, grad_points, grad_qkv, grad_proj, grad_gain, grad_bias = pl.pallas_call(
        deliver,
        out_shape=shapes,
        in_specs=[pl.BlockSpec(memory_space=pl.ANY)] * 6,
        out_specs=[hbm] * 6,
        scratch_shapes=[pltpu.SemaphoreType.DMA((6,))],
        compiler_params=pltpu.CompilerParams(vmem_limit_bytes=4 * 1024 * 1024),
    )(*results)
    return output[None], grad_points[None], grad_qkv.T, grad_proj.T, grad_gain[0], grad_bias[0]


def solution(mesh):
    placed = (
        P("group", "region", None),
        P("group", "region"),
        P("group", "region"),
        P("group", "region", None),
        P(),
        P(),
        P(),
        P(),
        P("group", "region", None),
    )
    return jax.shard_map(
        on_device,
        mesh=mesh,
        in_specs=placed,
        out_specs=(
            P("group", "region", None),
            P("group", "region", None),
            P("group", "region"),
            P("group", "region"),
            P(),
            P(),
        ),
        check_vma=False,
    )
```

```python
import jax
import jax.numpy as jnp
from jax import lax
from jax.experimental import pallas as pl
from jax.experimental.pallas import tpu as pltpu
from jax.sharding import PartitionSpec as P

HEAD_DIM = 16
EPS = 1e-05
PTS = 256
WIDTH = 512
CAP = 16
REGIONS = 32
GROUPS = 8
YS, ZS = 4, 8
CHUNK = 192
TOTAL = 65536
MESH = pl.DeviceIdType.MESH
BF = jnp.bfloat16
F32 = jnp.float32


def dot_nn(a, b):
    return jnp.dot(a, b, preferred_element_type=F32)


def dot_nt(a, b):
    return lax.dot_general(a, b, (((1,), (1,)), ((), ())), preferred_element_type=F32)


def as_column(row):
    return jnp.broadcast_to(row.astype(F32), (128, row.shape[1])).T.astype(jnp.int32)


def slot_rows(row):
    slots = lax.broadcasted_iota(jnp.int32, (REGIONS * CAP, PTS), 0)
    return jnp.where(slots == row, 1.0, 0.0).astype(BF)


def slot_columns(row):
    col = as_column(row)
    lane = lax.broadcasted_iota(jnp.int32, (PTS, 128), 1)
    parts = [jnp.where(col == lane + 128 * j, 1.0, 0.0) for j in range(4)]
    return jnp.concatenate(parts, axis=1).astype(BF)


def store_rows(ref, at, first, row):
    for j in range(4):
        ref[at, first + j : first + j + 1, :] = row[:, 128 * j : 128 * (j + 1)]


def load_row(block, first):
    return jnp.concatenate([block[first + j : first + j + 1, :] for j in range(4)], axis=1)


def kernel(
    x_hbm, rs_hbm, ps_hbm, pid_hbm, gain_hbm, bias_hbm, wqkv_hbm, wproj_hbm, cot_hbm,
    out_ref, gp_ref, gwq_ref, gwp_ref, gg_ref, gb_ref,
    x_ref, rs_ref, ps_ref, pid_ref, gain_ref, bias_ref, wqkv, wproj, cot_ref, in_sems,
    send_a, recv_a, send_b, recv_b, send_c, recv_c, send_d, recv_d,
    st1, st2, st3, gs1, gs2, gs3,
    p_t, q_n, q_t, aug_k, query_x, grad_x,
    unit_s, serial, qkv, qs, kt, value_x, score, es, heads, mixed_f, mixed_t, mixed,
    g_serial_t, gm, big_d, stack_g, stack_q, gqkv, left,
    right_s, right_m, own, g_core, r_core, s_x, r_x, s_y, r_y, s_z, r_z,
    send_sems, recv_sems, core_send, core_recv, x_send, x_recv, y_send, y_recv,
):
    r = lax.axis_index("region")
    g = lax.axis_index("group")
    xx, core = g // 2, g % 2
    yy, zz = r // ZS, r % ZS

    def each_region(act, first=1, end=REGIONS):
        def body(k, carry):
            act(lax.rem(r + k, REGIONS))
            return carry

        lax.fori_loop(first, end, body, 0)

    def each_group(act):
        def body(k, carry):
            act(lax.rem(g + k, GROUPS))
            return carry

        lax.fori_loop(1, GROUPS, body, 0)

    def remote(src, dst, send_sem, recv_sem, to):
        pltpu.make_async_remote_copy(
            src_ref=src, dst_ref=dst, send_sem=send_sem, recv_sem=recv_sem,
            device_id=to, device_id_type=MESH,
        ).start()

    def send(src, dst, stage, to):
        remote(src, dst, send_sems.at[stage], recv_sems.at[stage], to)

    def wait(ref, sem):
        pltpu.make_async_copy(ref, ref, sem).wait()

    def along_y(buf, stage):
        for k in range(1, YS):
            yp = lax.rem(yy + k, YS)
            send(buf.at[yy], buf.at[yy], stage, (yp * ZS + zz, g))

    def along_z(buf, stage):
        for k in range(1, ZS):
            zp = lax.rem(zz + k, ZS)
            send(buf.at[zz], buf.at[zz], stage, (yy * ZS + zp, g))

    def others(buf):
        return buf.at[pl.ds(0, buf.shape[0] - 1)]

    barrier = pltpu.get_barrier_semaphore()
    each_region(
        lambda p: pl.semaphore_signal(barrier, inc=1, device_id=(p, g), device_id_type=MESH)
    )
    each_group(
        lambda p: pl.semaphore_signal(barrier, inc=1, device_id=(r, p), device_id_type=MESH)
    )
    loads = [
        pltpu.make_async_copy(src, dst, in_sems.at[i])
        for i, (src, dst) in enumerate(
            [
                (rs_hbm, rs_ref), (x_hbm, x_ref), (ps_hbm, ps_ref), (pid_hbm, pid_ref),
                (cot_hbm, cot_ref), (gain_hbm, gain_ref), (bias_hbm, bias_ref),
                (wqkv_hbm, wqkv), (wproj_hbm, wproj),
            ]
        )
    ]
    for load in loads:
        load.start()

    loads[0].wait()
    p_n = slot_rows(rs_ref[...])
    loads[1].wait()
    x = x_ref[...]
    send_a[...] = dot_nn(p_n, x).astype(BF).reshape(REGIONS, CAP, WIDTH)

    pl.semaphore_wait(barrier, REGIONS - 1 + GROUPS - 1)

    each_region(lambda p: send(send_a.at[p], recv_a.at[r], 1, (p, g)))
    recv_a[r] = send_a[r]

    xf = x.astype(F32)
    mean_l = jnp.sum(xf, axis=0, keepdims=True) * (1.0 / PTS)
    dev = xf - mean_l
    store_rows(st1, g, 0, mean_l)
    store_rows(st1, g, 4, jnp.sum(dev * dev, axis=0, keepdims=True))
    each_group(lambda p: send(st1.at[g], st1.at[g], 0, (r, p)))

    for load in loads[2:]:
        load.wait()
    p_t[...] = slot_columns(rs_ref[...])
    q_n[...] = slot_rows(ps_ref[...])
    q_t[...] = slot_columns(ps_ref[...])
    send_b[...] = dot_nn(p_n, cot_ref[...]).astype(BF).reshape(REGIONS, CAP, WIDTH)
    pid_row = pid_ref[...]
    lane = lax.broadcasted_iota(jnp.int32, (PTS, 128), 1)
    aug_k[...] = jnp.where(
        (lane < 4) & (as_column(pid_row) != lane), -1e30, 0.0
    ).astype(BF)
    row = lax.broadcasted_iota(jnp.int32, (128, PTS), 0)
    same = jnp.where(row == pid_row, 1.0, 0.0).astype(BF)
    for j in range(4):
        query_x[j, 128:256, :] = same

    def merge(block, count, each):
        means, squares = block[:, 0:4, :], block[:, 4:8, :]
        mean = jnp.sum(means, axis=0) * (1.0 / count)
        off = means - mean[None]
        return mean, jnp.sum(squares, axis=0) + each * jnp.sum(off * off, axis=0)

    wait(others(st1), recv_sems.at[0])
    st2[yy, 0:4, :], st2[yy, 4:8, :] = merge(st1[...], GROUPS, float(PTS))
    along_y(st2, 2)
    wait(others(st2), recv_sems.at[2])
    st3[zz, 0:4, :], st3[zz, 4:8, :] = merge(st2[...], YS, float(PTS * GROUPS))
    along_z(st3, 9)

    each_region(lambda p: send(send_b.at[p], recv_b.at[r], 3, (p, g)))
    recv_b[r] = send_b[r]

    wait(others(st3), recv_sems.at[9])
    mean_4, square_4 = merge(st3[...], ZS, float(PTS * GROUPS * YS))
    inv_4 = lax.rsqrt(square_4 * (1.0 / TOTAL) + EPS)
    mean_all = load_row(mean_4, 0)
    inv_std = load_row(inv_4, 0)
    gain = gain_ref[...]

    wait(others(recv_a), recv_sems.at[1])
    pts = dot_nn(q_t[...], recv_a[...].reshape(REGIONS * CAP, WIDTH))
    unit = (pts - mean_all) * inv_std
    unit_s[...] = unit
    serial[...] = (unit * gain + bias_ref[...]).astype(BF)

    qkv[...] = dot_nn(serial[...], wqkv[...]).astype(BF)
    qs[...] = qkv[:, 0:WIDTH] * jnp.asarray(0.25, BF)
    kt[...] = qkv[:, WIDTH : 2 * WIDTH].T
    query_x[:, 0:128, :] = qs[...].T.reshape(4, 128, PTS)
    value_x[:, 0:HEAD_DIM, :] = qkv[:, 2 * WIDTH : 3 * WIDTH].T.reshape(32, HEAD_DIM, PTS)
    value_x[:, HEAD_DIM : 2 * HEAD_DIM, :] = jnp.ones((32, HEAD_DIM, PTS), BF)

    lane_1 = lax.broadcasted_iota(jnp.int32, (1, 128), 1)

    def head_mask(h):
        return jnp.where(lane_1 // HEAD_DIM == h, 1.0, 0.0).astype(BF)

    def forward(chunk, carry):
        col = pl.multiple_of(chunk * 128, 128)
        keys = qkv[:, pl.ds(WIDTH + col, 128)]
        for h in range(8):
            lhs = jnp.concatenate([keys * head_mask(h), aug_k[...]], axis=1)
            score[h] = dot_nn(lhs, query_x[chunk])
        for h in range(8):
            top = jnp.max(score[h], axis=0, keepdims=True)
            es[chunk, :, PTS * h : PTS * (h + 1)] = jnp.exp(score[h] - top).astype(BF)
        for h in range(8):
            e = es[chunk, :, PTS * h : PTS * (h + 1)]
            heads[chunk * 8 + h] = dot_nn(value_x[chunk * 8 + h], e)
        return carry

    lax.fori_loop(0, 4, forward, 0)
    inv_sum = 1.0 / heads[:, HEAD_DIM : HEAD_DIM + 1, :]
    mixed_f[...] = heads[:, 0:HEAD_DIM, :] * inv_sum
    mixed_t[...] = mixed_f[...].reshape(WIDTH, PTS).astype(BF)
    mixed[...] = mixed_t[...].T
    branch = dot_nn(mixed[...], wproj[...]).astype(BF)
    send_c[...] = dot_nn(q_n[...], branch).astype(BF).reshape(REGIONS, CAP, WIDTH)

    sibling = (r, xx * 2 + 1 - core)
    low_lanes = lax.broadcasted_iota(jnp.int32, (1, WIDTH), 1) % 128 < 64

    def packed(ref, source):
        rows = source.astype(F32)
        none = jnp.zeros_like(rows)
        for c, turn in ((0, 64), (1, WIDTH - 64)):
            turned = pltpu.roll(rows, turn, 1)
            first, second = (rows, turned) if c == 0 else (turned, rows)
            ref[c, 0:PTS, :] = jnp.where(low_lanes, first, none).astype(BF)
            ref[c, PTS : 2 * PTS, :] = jnp.where(low_lanes, none, second).astype(BF)

    def to_sibling(units, right, at, rows, slot):
        span = pl.ds(at, rows)
        own[span, :] = dot_nn(units, right[core])
        g_core[span, :] = dot_nn(units, right[1 - core]).astype(BF)
        remote(g_core.at[span], r_core.at[span], core_send.at[slot], core_recv.at[slot], sibling)

    def unit_pairs(rows, swap):
        by_unit = rows.reshape(rows.shape[0] // 32, 2, 16, PTS)
        halves = [by_unit[:, k].reshape(rows.shape[0] // 2, PTS) for k in range(2)]
        return jnp.concatenate(halves[::-1] if swap else halves, axis=1)

    def to_chips(at, rows, slot):
        span = pl.ds(at, rows)
        wait(r_core.at[span], core_recv.at[slot])
        both = own[span, :] + r_core[span, :].astype(F32)
        for b in range(4):
            s_x[b, span, :] = both[:, 128 * b : 128 * (b + 1)].astype(BF)
        for k in range(1, 4):
            xp = lax.rem(xx + k, 4)
            remote(
                s_x.at[xp, span], r_x.at[xx, span], x_send.at[slot], x_recv.at[slot],
                (r, xp * 2 + core),
            )

    packed(right_s, serial[...])
    packed(right_m, mixed[...])

    wait(others(recv_b), recv_sems.at[3])
    each_region(lambda p: send(send_c.at[p], recv_c.at[r], 4, (p, g)))
    recv_c[r] = send_c[r]
    g_serial = dot_nn(q_t[...], recv_b[...].reshape(REGIONS * CAP, WIDTH)).astype(BF)
    g_serial_t[...] = g_serial.T
    to_sibling(unit_pairs(g_serial_t[...], True), right_m, 4 * CHUNK, 256, 4)

    scaled = (
        dot_nn(wproj[...], g_serial_t[...]).reshape(32, HEAD_DIM, PTS) * inv_sum
    ).astype(BF)
    grad_x[:, 0:128, :] = scaled.reshape(4, 128, PTS)
    gm[...] = scaled.reshape(WIDTH, PTS).T
    inner = -jnp.sum(scaled.astype(F32) * mixed_f[...], axis=1, keepdims=True)
    first = inner.astype(BF).astype(F32)
    second = (inner - first).astype(BF).astype(F32)
    third = inner - first - second
    place = lax.broadcasted_iota(jnp.int32, (32, HEAD_DIM, PTS), 1)
    terms = jnp.where(
        place == 0, first, jnp.where(place == 1, second, jnp.where(place == 2, third, 0.0))
    )
    grad_x[:, 128:256, :] = terms.astype(BF).reshape(4, 128, PTS)

    def backward(chunk, carry):
        col = pl.multiple_of(chunk * 128, 128)
        values = qkv[:, pl.ds(2 * WIDTH + col, 128)]
        grads = gm[:, pl.ds(col, 128)]
        queries = qs[:, pl.ds(col, 128)]
        spans = [slice(PTS * h, PTS * (h + 1)) for h in range(8)]
        for h in range(8):
            stack_g[spans[h], :] = grads * head_mask(h)
            stack_q[spans[h], :] = queries * head_mask(h)
        for h in range(8):
            chosen = jnp.where(
                (lane_1 // HEAD_DIM == h) & (lane_1 % HEAD_DIM < 3), 1.0, 0.0
            ).astype(BF)
            lhs = jnp.concatenate(
                [values * head_mask(h), jnp.broadcast_to(chosen, (PTS, 128))], axis=1
            )
            ds = dot_nn(lhs, grad_x[chunk]).astype(BF) * es[chunk, :, spans[h]]
            big_d[:, spans[h]] = ds
        for h in range(8):
            rows = pl.ds(pl.multiple_of(col + HEAD_DIM * h, HEAD_DIM), HEAD_DIM)
            left[HEAD_DIM * h : HEAD_DIM * (h + 1), :] = (
                dot_nn(kt[rows, :], big_d[:, spans[h]]) * 0.25
            ).astype(BF)
        gqkv[:, pl.ds(col, 128)] = left[0:128, :].T
        gk = dot_nn(big_d[...], stack_q[...]).astype(BF)
        gqkv[:, pl.ds(WIDTH + col, 128)] = gk
        left[128:256, :] = gk.T
        gv = dot_nn(es[chunk], stack_g[...]).astype(BF)
        gqkv[:, pl.ds(2 * WIDTH + col, 128)] = gv
        left[256:384, :] = gv.T
        base = pl.multiple_of(chunk * CHUNK, 64)
        to_sibling(unit_pairs(left[...], False), right_s, base, CHUNK, chunk)

        @pl.when(chunk == 0)
        def _():
            to_chips(4 * CHUNK, 256, 4)

        @pl.when(chunk > 0)
        def _():
            to_chips(pl.multiple_of((chunk - 1) * CHUNK, 64), CHUNK, chunk - 1)

        return carry

    lax.fori_loop(0, 4, backward, 0)

    grad_in = dot_nt(gqkv[...], wqkv[...]).astype(BF)
    send_d[...] = dot_nn(q_n[...], grad_in).astype(BF).reshape(REGIONS, CAP, WIDTH)
    each_region(lambda p: send(send_d.at[p], recv_d.at[r], 7, (p, g)))
    recv_d[r] = send_d[r]
    to_chips(3 * CHUNK, CHUNK, 3)
    grad_f = grad_in.astype(F32)
    store_rows(gs1, g, 0, jnp.sum(grad_f, axis=0, keepdims=True))
    store_rows(gs1, g, 4, jnp.sum(grad_f * unit_s[...], axis=0, keepdims=True))
    each_group(lambda p: send(gs1.at[g], gs1.at[g], 6, (r, p)))

    def gather_chips(at, rows, slot):
        wait(r_x.at[pl.ds(0, 3), pl.ds(at, rows)], x_recv.at[slot])
        span = slice(at, at + rows)
        mine = pl.ds(pl.multiple_of(xx * 128, 128), 128)
        total = own[span, mine] + r_core[span, mine].astype(F32)
        for k in range(1, 4):
            total = total + r_x[lax.rem(xx + k, 4), span, :].astype(F32)
        return total.astype(BF)

    def to_y(at, owner, row, slot):
        remote(
            s_y.at[pl.ds(at, 64)], r_y.at[yy, pl.ds(row, 64)], y_send.at[0], y_recv.at[slot],
            (owner * ZS + zz, g),
        )

    def chunk_to_y(j):
        total = gather_chips(j * CHUNK, CHUNK, j)
        for p in range(3):
            b = p * 4 + j
            s_y[64 * b : 64 * (b + 1), :] = total[64 * p : 64 * (p + 1), :]

            @pl.when(yy != b // 3)
            def _():
                to_y(64 * b, b // 3, 64 * (b % 3), b % 3)

    s_y[768:1024, :] = gather_chips(4 * CHUNK, 256, 4)
    for k in range(1, YS):
        yp = lax.rem(yy + k, YS)
        to_y(pl.multiple_of(768 + yp * 64, 64), yp, 192, 3)
    chunk_to_y(0)

    wait(others(gs1), recv_sems.at[6])
    gs2[yy] = jnp.sum(gs1[...], axis=0)
    along_y(gs2, 8)
    chunk_to_y(1)

    wait(others(recv_c), recv_sems.at[4])
    out_ref[...] = dot_nn(p_t[...], recv_c[...].reshape(REGIONS * CAP, WIDTH)).astype(BF)

    wait(others(gs2), recv_sems.at[8])
    gs3[zz] = jnp.sum(gs2[...], axis=0)
    along_z(gs3, 5)

    chunk_to_y(2)
    chunk_to_y(3)
    for m in range(3):
        at = pl.multiple_of((yy * 3 + m) * 64, 64)
        r_y[yy, 64 * m : 64 * (m + 1), :] = s_y[pl.ds(at, 64), :]
    r_y[yy, 192:256, :] = s_y[pl.ds(pl.multiple_of(768 + yy * 64, 64), 64), :]
    for slot in range(4):
        wait(r_y.at[pl.ds(0, 3), pl.ds(64 * slot, 64)], y_recv.at[slot])
    over_y = jnp.sum(r_y[...].astype(F32), axis=0).astype(BF)
    low = low_lanes[:, 0:128]

    def rows_of(unit):
        return over_y[16 * unit : 16 * (unit + 1), :]

    for z in range(ZS):
        half = z // 2
        middle, proj = rows_of(3 * half + 1).astype(F32), rows_of(12 + half).astype(F32)
        s_z[z, 0:16, :] = rows_of(3 * half + 2 * (z % 2))
        mixed_rows = jnp.where(low, proj, middle) if z % 2 else jnp.where(low, middle, proj)
        s_z[z, 16:32, :] = mixed_rows.astype(BF)
    for k in range(1, ZS):
        zp = lax.rem(zz + k, ZS)
        send(s_z.at[zp], r_z.at[zz], 10, (yy * ZS + zp, g))
    r_z[zz] = s_z[zz]

    wait(others(gs3), recv_sems.at[5])
    sums = jnp.sum(gs3[...], axis=0)
    grad_bias = load_row(sums, 0)
    grad_gain = load_row(sums, 4)
    gb_ref[...] = grad_bias
    gg_ref[...] = grad_gain

    wait(others(recv_d), recv_sems.at[7])
    grad_n = dot_nn(p_t[...], recv_d[...].reshape(REGIONS * CAP, WIDTH))
    unit_b = (x_ref[...].astype(F32) - mean_all) * inv_std
    scale = 1.0 / TOTAL
    gp_ref[...] = (
        inv_std
        * (grad_n * gain - gain * grad_bias * scale - unit_b * (gain * grad_gain * scale))
    ).astype(BF)

    wait(others(r_z), recv_sems.at[10])
    final = jnp.sum(r_z[...].astype(F32), axis=0)
    even = zz % 2 == 0
    a, b = final[0:16, 0:64], final[0:16, 64:128]
    c, d = final[16:32, 0:64], final[16:32, 64:128]
    gwq_ref[0:16, :] = jnp.where(even, a, d)
    gwq_ref[16:32, :] = jnp.where(even, b, a)
    gwq_ref[32:48, :] = jnp.where(even, c, b)
    gwp_ref[...] = jnp.where(even, d, c)

    for buf, stage in (
        (st1, 0), (send_a, 1), (st2, 2), (send_b, 3), (send_c, 4), (gs3, 5), (gs1, 6),
        (send_d, 7), (gs2, 8), (st3, 9), (r_z, 10),
    ):
        wait(others(buf), send_sems.at[stage])
    wait(s_y.at[pl.ds(0, 768)], y_send.at[0])
    for slot, at, rows in [(j, j * CHUNK, CHUNK) for j in range(4)] + [(4, 4 * CHUNK, 256)]:
        wait(g_core.at[pl.ds(at, rows)], core_send.at[slot])
        wait(s_x.at[pl.ds(0, 3), pl.ds(at, rows)], x_send.at[slot])


def deliver(*refs):
    n = len(refs) // 2
    sems = refs[-1]
    copies = [pltpu.make_async_copy(refs[i], refs[n + i], sems.at[i]) for i in range(n)]
    for copy in copies:
        copy.start()
    for copy in copies:
        copy.wait()


def on_device(points, row_slot, pos_slot, patch_ids, bn_gain, bn_bias, w_qkv, w_proj, cotangent):
    vmem = pl.BlockSpec(memory_space=pltpu.VMEM)
    hbm = pl.BlockSpec(memory_space=pltpu.HBM)
    args = tuple(pltpu.with_memory_space_constraint(a, pltpu.HBM) for a in (
        points[0], row_slot, pos_slot, patch_ids[0], bn_gain[None], bn_bias[None],
        w_qkv, w_proj, cotangent[0],
    ))

    def buf(dtype, *shape):
        return pltpu.VMEM(shape, dtype)

    scratch = [buf(a.dtype, *a.shape) for a in args]
    scratch += [pltpu.SemaphoreType.DMA((9,))]
    scratch += [buf(BF, REGIONS, CAP, WIDTH) for _ in range(8)]
    scratch += [buf(F32, n, 8, 128) for n in (GROUPS, YS, ZS, GROUPS, YS, ZS)]
    scratch += [
        buf(BF, PTS, WIDTH),
        buf(BF, WIDTH, PTS),
        buf(BF, PTS, WIDTH),
        buf(BF, PTS, 128),
        buf(BF, 4, 256, PTS),
        buf(BF, 4, 256, PTS),
        buf(F32, PTS, WIDTH),
        buf(BF, PTS, WIDTH),
        buf(BF, PTS, 3 * WIDTH),
        buf(BF, PTS, WIDTH),
        buf(BF, WIDTH, PTS),
        buf(BF, 32, 2 * HEAD_DIM, PTS),
        buf(F32, 8, PTS, PTS),
        buf(BF, 4, PTS, 8 * PTS),
        buf(F32, 32, 2 * HEAD_DIM, PTS),
        buf(F32, 32, HEAD_DIM, PTS),
        buf(BF, WIDTH, PTS),
        buf(BF, PTS, WIDTH),
        buf(BF, WIDTH, PTS),
        buf(BF, PTS, WIDTH),
        buf(BF, PTS, 8 * PTS),
        buf(BF, 8 * PTS, 128),
        buf(BF, 8 * PTS, 128),
        buf(BF, PTS, 3 * WIDTH),
        buf(BF, 384, PTS),
        buf(BF, 2, 2 * PTS, WIDTH),
        buf(BF, 2, 2 * PTS, WIDTH),
        buf(F32, 1024, WIDTH),
        buf(BF, 1024, WIDTH),
        buf(BF, 1024, WIDTH),
        buf(BF, 4, 1024, 128),
        buf(BF, 4, 1024, 128),
        buf(BF, 1024, 128),
        buf(BF, YS, 256, 128),
        buf(BF, ZS, 32, 128),
        buf(BF, ZS, 32, 128),
    ]
    scratch += [pltpu.SemaphoreType.DMA((n,)) for n in (11, 11, 5, 5, 5, 5, 1, 4)]
    shapes = [
        jax.ShapeDtypeStruct((PTS, WIDTH), BF),
        jax.ShapeDtypeStruct((PTS, WIDTH), BF),
        jax.ShapeDtypeStruct((48, 64), F32),
        jax.ShapeDtypeStruct((16, 64), F32),
        jax.ShapeDtypeStruct((1, WIDTH), F32),
        jax.ShapeDtypeStruct((1, WIDTH), F32),
    ]
    results = pl.pallas_call(
        kernel,
        out_shape=shapes,
        in_specs=[hbm] * 9,
        out_specs=[vmem] * 6,
        scratch_shapes=scratch,
        compiler_params=pltpu.CompilerParams(
            collective_id=0, has_side_effects=True, vmem_limit_bytes=52 * 1024 * 1024
        ),
    )(*args)
    output, grad_points, grad_qkv, grad_proj, grad_gain, grad_bias = pl.pallas_call(
        deliver,
        out_shape=shapes,
        in_specs=[pl.BlockSpec(memory_space=pl.ANY)] * 6,
        out_specs=[hbm] * 6,
        scratch_shapes=[pltpu.SemaphoreType.DMA((6,))],
        compiler_params=pltpu.CompilerParams(vmem_limit_bytes=4 * 1024 * 1024),
    )(*results)
    return output[None], grad_points[None], grad_qkv.T, grad_proj.T, grad_gain[0], grad_bias[0]


def solution(mesh):
    placed = (
        P("group", "region", None),
        P("group", "region"),
        P("group", "region"),
        P("group", "region", None),
        P(),
        P(),
        P(),
        P(),
        P("group", "region", None),
    )
    return jax.shard_map(
        on_device,
        mesh=mesh,
        in_specs=placed,
        out_specs=(
            P("group", "region", None),
            P("group", "region", None),
            P("group", "region"),
            P("group", "region"),
            P(),
            P(),
        ),
        check_vma=False,
    )
```

```python
import jax
import jax.numpy as jnp
from jax import lax
from jax.experimental import pallas as pl
from jax.experimental.pallas import tpu as pltpu
from jax.sharding import PartitionSpec as P

HEAD_DIM = 16
EPS = 1e-05
PTS = 256
WIDTH = 512
CAP = 16
REGIONS = 32
GROUPS = 8
YS, ZS = 4, 8
CHUNK = 192
TOTAL = 65536
MESH = pl.DeviceIdType.MESH
BF = jnp.bfloat16
F32 = jnp.float32


def dot_nn(a, b):
    return jnp.dot(a, b, preferred_element_type=F32)


def dot_nt(a, b):
    return lax.dot_general(a, b, (((1,), (1,)), ((), ())), preferred_element_type=F32)


def as_column(row):
    return jnp.broadcast_to(row.astype(F32), (128, row.shape[1])).T.astype(jnp.int32)


def slot_rows(row):
    slots = lax.broadcasted_iota(jnp.int32, (REGIONS * CAP, PTS), 0)
    return jnp.where(slots == row, 1.0, 0.0).astype(BF)


def slot_columns(row):
    col = as_column(row)
    lane = lax.broadcasted_iota(jnp.int32, (PTS, 128), 1)
    parts = [jnp.where(col == lane + 128 * j, 1.0, 0.0) for j in range(4)]
    return jnp.concatenate(parts, axis=1).astype(BF)


def store_rows(ref, at, first, row):
    for j in range(4):
        ref[at, first + j : first + j + 1, :] = row[:, 128 * j : 128 * (j + 1)]


def load_row(block, first):
    return jnp.concatenate([block[first + j : first + j + 1, :] for j in range(4)], axis=1)


def kernel(
    x_hbm, rs_hbm, ps_hbm, pid_hbm, gain_hbm, bias_hbm, wqkv_hbm, wproj_hbm, cot_hbm,
    out_ref, gp_ref, gwq_ref, gwp_ref, gg_ref, gb_ref,
    x_ref, rs_ref, ps_ref, pid_ref, gain_ref, bias_ref, wqkv, wproj, cot_ref, in_sems,
    send_a, recv_a, send_b, recv_b, send_c, recv_c, send_d, recv_d,
    st1, st2, st3, gs1, gs2, gs3,
    p_t, q_n, q_t, aug_k, query_x, grad_x,
    unit_s, serial, qkv, qs, kt, value_x, score, es, heads, mixed_f, mixed_t, mixed,
    g_serial_t, gm, big_d, stack_g, stack_q, gqkv, left,
    right_s, right_m, own, g_core, r_core, s_x, r_x, s_y, r_y, s_z, r_z,
    send_sems, recv_sems, core_send, core_recv, x_send, x_recv, y_send, y_recv,
):
    r = lax.axis_index("region")
    g = lax.axis_index("group")
    xx, core = g // 2, g % 2
    yy, zz = r // ZS, r % ZS

    def each_region(act, first=1, end=REGIONS):
        def body(k, carry):
            act(lax.rem(r + k, REGIONS))
            return carry

        lax.fori_loop(first, end, body, 0)

    def each_group(act):
        def body(k, carry):
            act(lax.rem(g + k, GROUPS))
            return carry

        lax.fori_loop(1, GROUPS, body, 0)

    def remote(src, dst, send_sem, recv_sem, to):
        pltpu.make_async_remote_copy(
            src_ref=src, dst_ref=dst, send_sem=send_sem, recv_sem=recv_sem,
            device_id=to, device_id_type=MESH,
        ).start()

    def send(src, dst, stage, to):
        remote(src, dst, send_sems.at[stage], recv_sems.at[stage], to)

    def wait(ref, sem):
        pltpu.make_async_copy(ref, ref, sem).wait()

    def along_y(buf, stage):
        for k in range(1, YS):
            yp = lax.rem(yy + k, YS)
            send(buf.at[yy], buf.at[yy], stage, (yp * ZS + zz, g))

    def along_z(buf, stage):
        for k in range(1, ZS):
            zp = lax.rem(zz + k, ZS)
            send(buf.at[zz], buf.at[zz], stage, (yy * ZS + zp, g))

    def others(buf):
        return buf.at[pl.ds(0, buf.shape[0] - 1)]

    barrier = pltpu.get_barrier_semaphore()
    each_region(
        lambda p: pl.semaphore_signal(barrier, inc=1, device_id=(p, g), device_id_type=MESH)
    )
    each_group(
        lambda p: pl.semaphore_signal(barrier, inc=1, device_id=(r, p), device_id_type=MESH)
    )
    loads = [
        pltpu.make_async_copy(src, dst, in_sems.at[i])
        for i, (src, dst) in enumerate(
            [
                (rs_hbm, rs_ref), (x_hbm, x_ref), (ps_hbm, ps_ref), (pid_hbm, pid_ref),
                (cot_hbm, cot_ref), (gain_hbm, gain_ref), (bias_hbm, bias_ref),
                (wqkv_hbm, wqkv), (wproj_hbm, wproj),
            ]
        )
    ]
    for load in loads:
        load.start()

    loads[0].wait()
    p_n = slot_rows(rs_ref[...])
    loads[1].wait()
    x = x_ref[...]
    send_a[...] = dot_nn(p_n, x).astype(BF).reshape(REGIONS, CAP, WIDTH)

    pl.semaphore_wait(barrier, REGIONS - 1 + GROUPS - 1)

    each_region(lambda p: send(send_a.at[p], recv_a.at[r], 1, (p, g)))
    recv_a[r] = send_a[r]

    xf = x.astype(F32)
    mean_l = jnp.sum(xf, axis=0, keepdims=True) * (1.0 / PTS)
    dev = xf - mean_l
    store_rows(st1, g, 0, mean_l)
    store_rows(st1, g, 4, jnp.sum(dev * dev, axis=0, keepdims=True))
    each_group(lambda p: send(st1.at[g], st1.at[g], 0, (r, p)))

    for load in loads[2:]:
        load.wait()
    p_t[...] = slot_columns(rs_ref[...])
    q_n[...] = slot_rows(ps_ref[...])
    q_t[...] = slot_columns(ps_ref[...])
    send_b[...] = dot_nn(p_n, cot_ref[...]).astype(BF).reshape(REGIONS, CAP, WIDTH)
    pid_row = pid_ref[...]
    lane = lax.broadcasted_iota(jnp.int32, (PTS, 128), 1)
    aug_k[...] = jnp.where(
        (lane < 4) & (as_column(pid_row) != lane), -1e30, 0.0
    ).astype(BF)
    row = lax.broadcasted_iota(jnp.int32, (128, PTS), 0)
    same = jnp.where(row == pid_row, 1.0, 0.0).astype(BF)
    for j in range(4):
        query_x[j, 128:256, :] = same

    def merge(block, count, each):
        means, squares = block[:, 0:4, :], block[:, 4:8, :]
        mean = jnp.sum(means, axis=0) * (1.0 / count)
        off = means - mean[None]
        return mean, jnp.sum(squares, axis=0) + each * jnp.sum(off * off, axis=0)

    wait(others(st1), recv_sems.at[0])
    st2[yy, 0:4, :], st2[yy, 4:8, :] = merge(st1[...], GROUPS, float(PTS))
    along_y(st2, 2)
    wait(others(st2), recv_sems.at[2])
    st3[zz, 0:4, :], st3[zz, 4:8, :] = merge(st2[...], YS, float(PTS * GROUPS))
    along_z(st3, 9)

    each_region(lambda p: send(send_b.at[p], recv_b.at[r], 3, (p, g)))
    recv_b[r] = send_b[r]

    wait(others(st3), recv_sems.at[9])
    mean_4, square_4 = merge(st3[...], ZS, float(PTS * GROUPS * YS))
    inv_4 = lax.rsqrt(square_4 * (1.0 / TOTAL) + EPS)
    mean_all = load_row(mean_4, 0)
    inv_std = load_row(inv_4, 0)
    gain = gain_ref[...]

    wait(others(recv_a), recv_sems.at[1])
    pts = dot_nn(q_t[...], recv_a[...].reshape(REGIONS * CAP, WIDTH))
    unit = (pts - mean_all) * inv_std
    unit_s[...] = unit
    serial[...] = (unit * gain + bias_ref[...]).astype(BF)

    qkv[...] = dot_nn(serial[...], wqkv[...]).astype(BF)
    qs[...] = qkv[:, 0:WIDTH] * jnp.asarray(0.25, BF)
    kt[...] = qkv[:, WIDTH : 2 * WIDTH].T
    query_x[:, 0:128, :] = qs[...].T.reshape(4, 128, PTS)
    value_x[:, 0:HEAD_DIM, :] = qkv[:, 2 * WIDTH : 3 * WIDTH].T.reshape(32, HEAD_DIM, PTS)
    value_x[:, HEAD_DIM : 2 * HEAD_DIM, :] = jnp.ones((32, HEAD_DIM, PTS), BF)

    lane_1 = lax.broadcasted_iota(jnp.int32, (1, 128), 1)

    def head_mask(h):
        return jnp.where(lane_1 // HEAD_DIM == h, 1.0, 0.0).astype(BF)

    def forward(chunk, carry):
        col = pl.multiple_of(chunk * 128, 128)
        keys = qkv[:, pl.ds(WIDTH + col, 128)]
        for h in range(8):
            lhs = jnp.concatenate([keys * head_mask(h), aug_k[...]], axis=1)
            score[h] = dot_nn(lhs, query_x[chunk])
        for h in range(8):
            top = jnp.max(score[h], axis=0, keepdims=True)
            es[chunk, :, PTS * h : PTS * (h + 1)] = jnp.exp(score[h] - top).astype(BF)
        for h in range(8):
            e = es[chunk, :, PTS * h : PTS * (h + 1)]
            heads[chunk * 8 + h] = dot_nn(value_x[chunk * 8 + h], e)
        return carry

    lax.fori_loop(0, 4, forward, 0)
    inv_sum = 1.0 / heads[:, HEAD_DIM : HEAD_DIM + 1, :]
    mixed_f[...] = heads[:, 0:HEAD_DIM, :] * inv_sum
    mixed_t[...] = mixed_f[...].reshape(WIDTH, PTS).astype(BF)
    mixed[...] = mixed_t[...].T
    branch = dot_nn(mixed[...], wproj[...]).astype(BF)
    send_c[...] = dot_nn(q_n[...], branch).astype(BF).reshape(REGIONS, CAP, WIDTH)

    sibling = (r, xx * 2 + 1 - core)
    low_lanes = lax.broadcasted_iota(jnp.int32, (1, WIDTH), 1) % 128 < 64

    def packed(ref, source):
        rows = source.astype(F32)
        none = jnp.zeros_like(rows)
        for c, turn in ((0, 64), (1, WIDTH - 64)):
            turned = pltpu.roll(rows, turn, 1)
            first, second = (rows, turned) if c == 0 else (turned, rows)
            ref[c, 0:PTS, :] = jnp.where(low_lanes, first, none).astype(BF)
            ref[c, PTS : 2 * PTS, :] = jnp.where(low_lanes, none, second).astype(BF)

    def to_sibling(units, right, at, rows, slot):
        span = pl.ds(at, rows)
        own[span, :] = dot_nn(units, right[core])
        g_core[span, :] = dot_nn(units, right[1 - core]).astype(BF)
        remote(g_core.at[span], r_core.at[span], core_send.at[slot], core_recv.at[slot], sibling)

    def unit_pairs(rows, swap):
        by_unit = rows.reshape(rows.shape[0] // 32, 2, 16, PTS)
        halves = [by_unit[:, k].reshape(rows.shape[0] // 2, PTS) for k in range(2)]
        return jnp.concatenate(halves[::-1] if swap else halves, axis=1)

    def to_chips(at, rows, slot):
        span = pl.ds(at, rows)
        wait(r_core.at[span], core_recv.at[slot])
        both = own[span, :] + r_core[span, :].astype(F32)
        for b in range(4):
            s_x[b, span, :] = both[:, 128 * b : 128 * (b + 1)].astype(BF)
        for k in range(1, 4):
            xp = lax.rem(xx + k, 4)
            remote(
                s_x.at[xp, span], r_x.at[xx, span], x_send.at[slot], x_recv.at[slot],
                (r, xp * 2 + core),
            )

    packed(right_s, serial[...])
    packed(right_m, mixed[...])

    wait(others(recv_b), recv_sems.at[3])
    each_region(lambda p: send(send_c.at[p], recv_c.at[r], 4, (p, g)))
    recv_c[r] = send_c[r]
    g_serial = dot_nn(q_t[...], recv_b[...].reshape(REGIONS * CAP, WIDTH)).astype(BF)
    g_serial_t[...] = g_serial.T
    to_sibling(unit_pairs(g_serial_t[...], True), right_m, 4 * CHUNK, 256, 4)

    scaled = (
        dot_nn(wproj[...], g_serial_t[...]).reshape(32, HEAD_DIM, PTS) * inv_sum
    ).astype(BF)
    grad_x[:, 0:128, :] = scaled.reshape(4, 128, PTS)
    gm[...] = scaled.reshape(WIDTH, PTS).T
    inner = -jnp.sum(scaled.astype(F32) * mixed_f[...], axis=1, keepdims=True)
    first = inner.astype(BF).astype(F32)
    second = (inner - first).astype(BF).astype(F32)
    third = inner - first - second
    place = lax.broadcasted_iota(jnp.int32, (32, HEAD_DIM, PTS), 1)
    terms = jnp.where(
        place == 0, first, jnp.where(place == 1, second, jnp.where(place == 2, third, 0.0))
    )
    grad_x[:, 128:256, :] = terms.astype(BF).reshape(4, 128, PTS)

    def backward(chunk, carry):
        col = pl.multiple_of(chunk * 128, 128)
        values = qkv[:, pl.ds(2 * WIDTH + col, 128)]
        grads = gm[:, pl.ds(col, 128)]
        queries = qs[:, pl.ds(col, 128)]
        spans = [slice(PTS * h, PTS * (h + 1)) for h in range(8)]
        for h in range(8):
            stack_g[spans[h], :] = grads * head_mask(h)
            stack_q[spans[h], :] = queries * head_mask(h)
        for h in range(8):
            chosen = jnp.where(
                (lane_1 // HEAD_DIM == h) & (lane_1 % HEAD_DIM < 3), 1.0, 0.0
            ).astype(BF)
            lhs = jnp.concatenate(
                [values * head_mask(h), jnp.broadcast_to(chosen, (PTS, 128))], axis=1
            )
            ds = dot_nn(lhs, grad_x[chunk]).astype(BF) * es[chunk, :, spans[h]]
            big_d[:, spans[h]] = ds
        for h in range(8):
            rows = pl.ds(pl.multiple_of(col + HEAD_DIM * h, HEAD_DIM), HEAD_DIM)
            left[HEAD_DIM * h : HEAD_DIM * (h + 1), :] = (
                dot_nn(kt[rows, :], big_d[:, spans[h]]) * 0.25
            ).astype(BF)
        gqkv[:, pl.ds(col, 128)] = left[0:128, :].T
        gk = dot_nn(big_d[...], stack_q[...]).astype(BF)
        gqkv[:, pl.ds(WIDTH + col, 128)] = gk
        left[128:256, :] = gk.T
        gv = dot_nn(es[chunk], stack_g[...]).astype(BF)
        gqkv[:, pl.ds(2 * WIDTH + col, 128)] = gv
        left[256:384, :] = gv.T
        base = pl.multiple_of(chunk * CHUNK, 64)
        to_sibling(unit_pairs(left[...], False), right_s, base, CHUNK, chunk)

        @pl.when(chunk == 0)
        def _():
            to_chips(4 * CHUNK, 256, 4)

        @pl.when(chunk > 0)
        def _():
            to_chips(pl.multiple_of((chunk - 1) * CHUNK, 64), CHUNK, chunk - 1)

        return carry

    lax.fori_loop(0, 4, backward, 0)

    grad_in = dot_nt(gqkv[...], wqkv[...]).astype(BF)
    send_d[...] = dot_nn(q_n[...], grad_in).astype(BF).reshape(REGIONS, CAP, WIDTH)
    each_region(lambda p: send(send_d.at[p], recv_d.at[r], 7, (p, g)))
    recv_d[r] = send_d[r]
    to_chips(3 * CHUNK, CHUNK, 3)
    grad_f = grad_in.astype(F32)
    store_rows(gs1, g, 0, jnp.sum(grad_f, axis=0, keepdims=True))
    store_rows(gs1, g, 4, jnp.sum(grad_f * unit_s[...], axis=0, keepdims=True))
    each_group(lambda p: send(gs1.at[g], gs1.at[g], 6, (r, p)))

    def gather_chips(at, rows, slot):
        wait(r_x.at[pl.ds(0, 3), pl.ds(at, rows)], x_recv.at[slot])
        span = slice(at, at + rows)
        mine = pl.ds(pl.multiple_of(xx * 128, 128), 128)
        total = own[span, mine] + r_core[span, mine].astype(F32)
        for k in range(1, 4):
            total = total + r_x[lax.rem(xx + k, 4), span, :].astype(F32)
        return total.astype(BF)

    def to_y(at, owner, row, slot):
        remote(
            s_y.at[pl.ds(at, 64)], r_y.at[yy, pl.ds(row, 64)], y_send.at[0], y_recv.at[slot],
            (owner * ZS + zz, g),
        )

    def chunk_to_y(j):
        total = gather_chips(j * CHUNK, CHUNK, j)
        for p in range(3):
            b = p * 4 + j
            s_y[64 * b : 64 * (b + 1), :] = total[64 * p : 64 * (p + 1), :]

            @pl.when(yy != b // 3)
            def _():
                to_y(64 * b, b // 3, 64 * (b % 3), b % 3)

    s_y[768:1024, :] = gather_chips(4 * CHUNK, 256, 4)
    for k in range(1, YS):
        yp = lax.rem(yy + k, YS)
        to_y(pl.multiple_of(768 + yp * 64, 64), yp, 192, 3)
    chunk_to_y(0)

    chunk_to_y(1)

    wait(others(recv_c), recv_sems.at[4])
    out_ref[...] = dot_nn(p_t[...], recv_c[...].reshape(REGIONS * CAP, WIDTH)).astype(BF)


    chunk_to_y(2)
    wait(others(gs1), recv_sems.at[6])
    gs2[yy] = jnp.sum(gs1[...], axis=0)
    along_y(gs2, 8)
    chunk_to_y(3)
    for m in range(3):
        at = pl.multiple_of((yy * 3 + m) * 64, 64)
        r_y[yy, 64 * m : 64 * (m + 1), :] = s_y[pl.ds(at, 64), :]
    r_y[yy, 192:256, :] = s_y[pl.ds(pl.multiple_of(768 + yy * 64, 64), 64), :]
    for slot in range(4):
        wait(r_y.at[pl.ds(0, 3), pl.ds(64 * slot, 64)], y_recv.at[slot])
    over_y = jnp.sum(r_y[...].astype(F32), axis=0).astype(BF)
    low = low_lanes[:, 0:128]

    def rows_of(unit):
        return over_y[16 * unit : 16 * (unit + 1), :]

    for z in range(ZS):
        half = z // 2
        middle, proj = rows_of(3 * half + 1).astype(F32), rows_of(12 + half).astype(F32)
        s_z[z, 0:16, :] = rows_of(3 * half + 2 * (z % 2))
        mixed_rows = jnp.where(low, proj, middle) if z % 2 else jnp.where(low, middle, proj)
        s_z[z, 16:32, :] = mixed_rows.astype(BF)
    for k in range(1, ZS):
        zp = lax.rem(zz + k, ZS)
        send(s_z.at[zp], r_z.at[zz], 10, (yy * ZS + zp, g))
    r_z[zz] = s_z[zz]
    wait(others(gs2), recv_sems.at[8])
    gs3[zz] = jnp.sum(gs2[...], axis=0)
    along_z(gs3, 5)

    wait(others(recv_d), recv_sems.at[7])
    grad_n = dot_nn(p_t[...], recv_d[...].reshape(REGIONS * CAP, WIDTH))
    scaled_n = grad_n * (inv_std * gain)
    unit_b = (x_ref[...].astype(F32) - mean_all) * inv_std

    wait(others(gs3), recv_sems.at[5])
    sums = jnp.sum(gs3[...], axis=0)
    grad_bias = load_row(sums, 0)
    grad_gain = load_row(sums, 4)
    gb_ref[...] = grad_bias
    gg_ref[...] = grad_gain
    scale = inv_std * gain * (1.0 / TOTAL)
    gp_ref[...] = (scaled_n - scale * grad_bias - unit_b * (scale * grad_gain)).astype(BF)

    wait(others(r_z), recv_sems.at[10])
    final = jnp.sum(r_z[...].astype(F32), axis=0)
    even = zz % 2 == 0
    a, b = final[0:16, 0:64], final[0:16, 64:128]
    c, d = final[16:32, 0:64], final[16:32, 64:128]
    gwq_ref[0:16, :] = jnp.where(even, a, d)
    gwq_ref[16:32, :] = jnp.where(even, b, a)
    gwq_ref[32:48, :] = jnp.where(even, c, b)
    gwp_ref[...] = jnp.where(even, d, c)

    for buf, stage in (
        (st1, 0), (send_a, 1), (st2, 2), (send_b, 3), (send_c, 4), (gs3, 5), (gs1, 6),
        (send_d, 7), (gs2, 8), (st3, 9), (r_z, 10),
    ):
        wait(others(buf), send_sems.at[stage])
    wait(s_y.at[pl.ds(0, 768)], y_send.at[0])
    for slot, at, rows in [(j, j * CHUNK, CHUNK) for j in range(4)] + [(4, 4 * CHUNK, 256)]:
        wait(g_core.at[pl.ds(at, rows)], core_send.at[slot])
        wait(s_x.at[pl.ds(0, 3), pl.ds(at, rows)], x_send.at[slot])


def deliver(*refs):
    n = len(refs) // 2
    sems = refs[-1]
    copies = [pltpu.make_async_copy(refs[i], refs[n + i], sems.at[i]) for i in range(n)]
    for copy in copies:
        copy.start()
    for copy in copies:
        copy.wait()


def on_device(points, row_slot, pos_slot, patch_ids, bn_gain, bn_bias, w_qkv, w_proj, cotangent):
    vmem = pl.BlockSpec(memory_space=pltpu.VMEM)
    hbm = pl.BlockSpec(memory_space=pltpu.HBM)
    args = tuple(pltpu.with_memory_space_constraint(a, pltpu.HBM) for a in (
        points[0], row_slot, pos_slot, patch_ids[0], bn_gain[None], bn_bias[None],
        w_qkv, w_proj, cotangent[0],
    ))

    def buf(dtype, *shape):
        return pltpu.VMEM(shape, dtype)

    scratch = [buf(a.dtype, *a.shape) for a in args]
    scratch += [pltpu.SemaphoreType.DMA((9,))]
    scratch += [buf(BF, REGIONS, CAP, WIDTH) for _ in range(8)]
    scratch += [buf(F32, n, 8, 128) for n in (GROUPS, YS, ZS, GROUPS, YS, ZS)]
    scratch += [
        buf(BF, PTS, WIDTH),
        buf(BF, WIDTH, PTS),
        buf(BF, PTS, WIDTH),
        buf(BF, PTS, 128),
        buf(BF, 4, 256, PTS),
        buf(BF, 4, 256, PTS),
        buf(F32, PTS, WIDTH),
        buf(BF, PTS, WIDTH),
        buf(BF, PTS, 3 * WIDTH),
        buf(BF, PTS, WIDTH),
        buf(BF, WIDTH, PTS),
        buf(BF, 32, 2 * HEAD_DIM, PTS),
        buf(F32, 8, PTS, PTS),
        buf(BF, 4, PTS, 8 * PTS),
        buf(F32, 32, 2 * HEAD_DIM, PTS),
        buf(F32, 32, HEAD_DIM, PTS),
        buf(BF, WIDTH, PTS),
        buf(BF, PTS, WIDTH),
        buf(BF, WIDTH, PTS),
        buf(BF, PTS, WIDTH),
        buf(BF, PTS, 8 * PTS),
        buf(BF, 8 * PTS, 128),
        buf(BF, 8 * PTS, 128),
        buf(BF, PTS, 3 * WIDTH),
        buf(BF, 384, PTS),
        buf(BF, 2, 2 * PTS, WIDTH),
        buf(BF, 2, 2 * PTS, WIDTH),
        buf(F32, 1024, WIDTH),
        buf(BF, 1024, WIDTH),
        buf(BF, 1024, WIDTH),
        buf(BF, 4, 1024, 128),
        buf(BF, 4, 1024, 128),
        buf(BF, 1024, 128),
        buf(BF, YS, 256, 128),
        buf(BF, ZS, 32, 128),
        buf(BF, ZS, 32, 128),
    ]
    scratch += [pltpu.SemaphoreType.DMA((n,)) for n in (11, 11, 5, 5, 5, 5, 1, 4)]
    shapes = [
        jax.ShapeDtypeStruct((PTS, WIDTH), BF),
        jax.ShapeDtypeStruct((PTS, WIDTH), BF),
        jax.ShapeDtypeStruct((48, 64), F32),
        jax.ShapeDtypeStruct((16, 64), F32),
        jax.ShapeDtypeStruct((1, WIDTH), F32),
        jax.ShapeDtypeStruct((1, WIDTH), F32),
    ]
    results = pl.pallas_call(
        kernel,
        out_shape=shapes,
        in_specs=[hbm] * 9,
        out_specs=[vmem] * 6,
        scratch_shapes=scratch,
        compiler_params=pltpu.CompilerParams(
            collective_id=0, has_side_effects=True, vmem_limit_bytes=52 * 1024 * 1024
        ),
    )(*args)
    output, grad_points, grad_qkv, grad_proj, grad_gain, grad_bias = pl.pallas_call(
        deliver,
        out_shape=shapes,
        in_specs=[pl.BlockSpec(memory_space=pl.ANY)] * 6,
        out_specs=[hbm] * 6,
        scratch_shapes=[pltpu.SemaphoreType.DMA((6,))],
        compiler_params=pltpu.CompilerParams(vmem_limit_bytes=4 * 1024 * 1024),
    )(*results)
    return output[None], grad_points[None], grad_qkv.T, grad_proj.T, grad_gain[0], grad_bias[0]


def solution(mesh):
    placed = (
        P("group", "region", None),
        P("group", "region"),
        P("group", "region"),
        P("group", "region", None),
        P(),
        P(),
        P(),
        P(),
        P("group", "region", None),
    )
    return jax.shard_map(
        on_device,
        mesh=mesh,
        in_specs=placed,
        out_specs=(
            P("group", "region", None),
            P("group", "region", None),
            P("group", "region"),
            P("group", "region"),
            P(),
            P(),
        ),
        check_vma=False,
    )
```

```python
import jax
import jax.numpy as jnp
from jax import lax
from jax.experimental import pallas as pl
from jax.experimental.pallas import tpu as pltpu
from jax.sharding import PartitionSpec as P

HEAD_DIM = 16
EPS = 1e-05
PTS = 256
WIDTH = 512
CAP = 16
REGIONS = 32
GROUPS = 8
YS, ZS = 4, 8
CHUNK = 192
TOTAL = 65536
MESH = pl.DeviceIdType.MESH
BF = jnp.bfloat16
F32 = jnp.float32


def dot_nn(a, b):
    return jnp.dot(a, b, preferred_element_type=F32)


def dot_nt(a, b):
    return lax.dot_general(a, b, (((1,), (1,)), ((), ())), preferred_element_type=F32)


def as_column(row):
    return jnp.broadcast_to(row.astype(F32), (128, row.shape[1])).T.astype(jnp.int32)


def slot_rows(row):
    slots = lax.broadcasted_iota(jnp.int32, (REGIONS * CAP, PTS), 0)
    return jnp.where(slots == row, 1.0, 0.0).astype(BF)


def slot_columns(row):
    col = as_column(row)
    lane = lax.broadcasted_iota(jnp.int32, (PTS, 128), 1)
    parts = [jnp.where(col == lane + 128 * j, 1.0, 0.0) for j in range(4)]
    return jnp.concatenate(parts, axis=1).astype(BF)


def store_rows(ref, at, first, row):
    for j in range(4):
        ref[at, first + j : first + j + 1, :] = row[:, 128 * j : 128 * (j + 1)]


def load_row(block, first):
    return jnp.concatenate([block[first + j : first + j + 1, :] for j in range(4)], axis=1)


def kernel(
    x_hbm, rs_hbm, ps_hbm, pid_hbm, gain_hbm, bias_hbm, wqkv_hbm, wproj_hbm, cot_hbm,
    out_ref, gp_ref, gwq_ref, gwp_ref, gg_ref, gb_ref,
    x_ref, rs_ref, ps_ref, pid_ref, gain_ref, bias_ref, wqkv, wproj, cot_ref, in_sems,
    send_a, recv_a, send_b, recv_b, send_c, recv_c, send_d, recv_d,
    st1, st2, st3, gs1, gs2, gs3,
    p_t, q_n, q_t, aug_k, query_x, grad_x,
    unit_s, serial, qkv, qs, kt, value_x, score, es, heads, mixed_f, mixed_t, mixed,
    g_serial_t, gm, big_d, stack_g, stack_q, gqkv, left,
    right_s, right_m, own, g_core, r_core, s_x, r_x, s_y, r_y, s_z, r_z,
    send_sems, recv_sems, core_send, core_recv, x_send, x_recv, y_send, y_recv,
):
    r = lax.axis_index("region")
    g = lax.axis_index("group")
    xx, core = g // 2, g % 2
    yy, zz = r // ZS, r % ZS

    def each_region(act, first=1, end=REGIONS):
        def body(k, carry):
            act(lax.rem(r + k, REGIONS))
            return carry

        lax.fori_loop(first, end, body, 0)

    def each_group(act):
        def body(k, carry):
            act(lax.rem(g + k, GROUPS))
            return carry

        lax.fori_loop(1, GROUPS, body, 0)

    def remote(src, dst, send_sem, recv_sem, to):
        pltpu.make_async_remote_copy(
            src_ref=src, dst_ref=dst, send_sem=send_sem, recv_sem=recv_sem,
            device_id=to, device_id_type=MESH,
        ).start()

    def send(src, dst, stage, to):
        remote(src, dst, send_sems.at[stage], recv_sems.at[stage], to)

    def wait(ref, sem):
        pltpu.make_async_copy(ref, ref, sem).wait()

    def along_y(buf, stage):
        for k in range(1, YS):
            yp = lax.rem(yy + k, YS)
            send(buf.at[yy], buf.at[yy], stage, (yp * ZS + zz, g))

    def along_z(buf, stage):
        for k in range(1, ZS):
            zp = lax.rem(zz + k, ZS)
            send(buf.at[zz], buf.at[zz], stage, (yy * ZS + zp, g))

    def others(buf):
        return buf.at[pl.ds(0, buf.shape[0] - 1)]

    barrier = pltpu.get_barrier_semaphore()
    each_region(
        lambda p: pl.semaphore_signal(barrier, inc=1, device_id=(p, g), device_id_type=MESH)
    )
    each_group(
        lambda p: pl.semaphore_signal(barrier, inc=1, device_id=(r, p), device_id_type=MESH)
    )
    loads = [
        pltpu.make_async_copy(src, dst, in_sems.at[i])
        for i, (src, dst) in enumerate(
            [
                (rs_hbm, rs_ref), (x_hbm, x_ref), (ps_hbm, ps_ref), (pid_hbm, pid_ref),
                (cot_hbm, cot_ref), (gain_hbm, gain_ref), (bias_hbm, bias_ref),
                (wqkv_hbm, wqkv), (wproj_hbm, wproj),
            ]
        )
    ]
    for load in loads:
        load.start()

    loads[0].wait()
    p_n = slot_rows(rs_ref[...])
    loads[1].wait()
    x = x_ref[...]
    send_a[...] = dot_nn(p_n, x).astype(BF).reshape(REGIONS, CAP, WIDTH)

    pl.semaphore_wait(barrier, REGIONS - 1 + GROUPS - 1)

    each_region(lambda p: send(send_a.at[p], recv_a.at[r], 1, (p, g)))
    recv_a[r] = send_a[r]

    xf = x.astype(F32)
    mean_l = jnp.sum(xf, axis=0, keepdims=True) * (1.0 / PTS)
    dev = xf - mean_l
    store_rows(st1, g, 0, mean_l)
    store_rows(st1, g, 4, jnp.sum(dev * dev, axis=0, keepdims=True))
    each_group(lambda p: send(st1.at[g], st1.at[g], 0, (r, p)))

    for load in loads[2:]:
        load.wait()
    p_t[...] = slot_columns(rs_ref[...])
    q_n[...] = slot_rows(ps_ref[...])
    q_t[...] = slot_columns(ps_ref[...])
    send_b[...] = dot_nn(p_n, cot_ref[...]).astype(BF).reshape(REGIONS, CAP, WIDTH)
    pid_row = pid_ref[...]
    lane = lax.broadcasted_iota(jnp.int32, (PTS, 128), 1)
    aug_k[...] = jnp.where(
        (lane < 4) & (as_column(pid_row) != lane), -1e30, 0.0
    ).astype(BF)
    row = lax.broadcasted_iota(jnp.int32, (128, PTS), 0)
    same = jnp.where(row == pid_row, 1.0, 0.0).astype(BF)
    for j in range(4):
        query_x[j, 128:256, :] = same

    def merge(block, count, each):
        means, squares = block[:, 0:4, :], block[:, 4:8, :]
        mean = jnp.sum(means, axis=0) * (1.0 / count)
        off = means - mean[None]
        return mean, jnp.sum(squares, axis=0) + each * jnp.sum(off * off, axis=0)

    wait(others(st1), recv_sems.at[0])
    st2[yy, 0:4, :], st2[yy, 4:8, :] = merge(st1[...], GROUPS, float(PTS))
    along_y(st2, 2)
    wait(others(st2), recv_sems.at[2])
    st3[zz, 0:4, :], st3[zz, 4:8, :] = merge(st2[...], YS, float(PTS * GROUPS))
    along_z(st3, 9)

    each_region(lambda p: send(send_b.at[p], recv_b.at[r], 3, (p, g)))
    recv_b[r] = send_b[r]

    wait(others(st3), recv_sems.at[9])
    mean_4, square_4 = merge(st3[...], ZS, float(PTS * GROUPS * YS))
    inv_4 = lax.rsqrt(square_4 * (1.0 / TOTAL) + EPS)
    mean_all = load_row(mean_4, 0)
    inv_std = load_row(inv_4, 0)
    gain = gain_ref[...]

    wait(others(recv_a), recv_sems.at[1])
    pts = dot_nn(q_t[...], recv_a[...].reshape(REGIONS * CAP, WIDTH))
    unit = (pts - mean_all) * inv_std
    unit_s[...] = unit
    serial[...] = (unit * gain + bias_ref[...]).astype(BF)

    qkv[...] = dot_nn(serial[...], wqkv[...]).astype(BF)
    qs[...] = qkv[:, 0:WIDTH] * jnp.asarray(0.25, BF)
    kt[...] = qkv[:, WIDTH : 2 * WIDTH].T
    query_x[:, 0:128, :] = qs[...].T.reshape(4, 128, PTS)
    value_x[:, 0:HEAD_DIM, :] = qkv[:, 2 * WIDTH : 3 * WIDTH].T.reshape(32, HEAD_DIM, PTS)
    value_x[:, HEAD_DIM : 2 * HEAD_DIM, :] = jnp.ones((32, HEAD_DIM, PTS), BF)

    lane_1 = lax.broadcasted_iota(jnp.int32, (1, 128), 1)

    def head_mask(h):
        return jnp.where(lane_1 // HEAD_DIM == h, 1.0, 0.0).astype(BF)

    def forward(chunk, carry):
        col = pl.multiple_of(chunk * 128, 128)
        keys = qkv[:, pl.ds(WIDTH + col, 128)]
        for h in range(8):
            lhs = jnp.concatenate([keys * head_mask(h), aug_k[...]], axis=1)
            score[h] = dot_nn(lhs, query_x[chunk])
        for h in range(8):
            top = jnp.max(score[h], axis=0, keepdims=True)
            es[chunk, :, PTS * h : PTS * (h + 1)] = jnp.exp(score[h] - top).astype(BF)
        for h in range(8):
            e = es[chunk, :, PTS * h : PTS * (h + 1)]
            heads[chunk * 8 + h] = dot_nn(value_x[chunk * 8 + h], e)
        return carry

    lax.fori_loop(0, 4, forward, 0)
    inv_sum = 1.0 / heads[:, HEAD_DIM : HEAD_DIM + 1, :]
    mixed_f[...] = heads[:, 0:HEAD_DIM, :] * inv_sum
    mixed_t[...] = mixed_f[...].reshape(WIDTH, PTS).astype(BF)
    mixed[...] = mixed_t[...].T
    branch = dot_nn(mixed[...], wproj[...]).astype(BF)
    send_c[...] = dot_nn(q_n[...], branch).astype(BF).reshape(REGIONS, CAP, WIDTH)

    sibling = (r, xx * 2 + 1 - core)
    low_lanes = lax.broadcasted_iota(jnp.int32, (1, WIDTH), 1) % 128 < 64

    def packed(ref, source):
        rows = source.astype(F32)
        none = jnp.zeros_like(rows)
        for c, turn in ((0, 64), (1, WIDTH - 64)):
            turned = pltpu.roll(rows, turn, 1)
            first, second = (rows, turned) if c == 0 else (turned, rows)
            ref[c, 0:PTS, :] = jnp.where(low_lanes, first, none).astype(BF)
            ref[c, PTS : 2 * PTS, :] = jnp.where(low_lanes, none, second).astype(BF)

    def to_sibling(units, right, at, rows, slot):
        span = pl.ds(at, rows)
        own[span, :] = dot_nn(units, right[core])
        g_core[span, :] = dot_nn(units, right[1 - core]).astype(BF)
        remote(g_core.at[span], r_core.at[span], core_send.at[slot], core_recv.at[slot], sibling)

    def unit_pairs(rows, swap):
        by_unit = rows.reshape(rows.shape[0] // 32, 2, 16, PTS)
        halves = [by_unit[:, k].reshape(rows.shape[0] // 2, PTS) for k in range(2)]
        return jnp.concatenate(halves[::-1] if swap else halves, axis=1)

    def to_chips(at, rows, slot):
        span = pl.ds(at, rows)
        wait(r_core.at[span], core_recv.at[slot])
        both = own[span, :] + r_core[span, :].astype(F32)
        for b in range(4):
            s_x[b, span, :] = both[:, 128 * b : 128 * (b + 1)].astype(BF)
        for k in range(1, 4):
            xp = lax.rem(xx + k, 4)
            remote(
                s_x.at[xp, span], r_x.at[xx, span], x_send.at[slot], x_recv.at[slot],
                (r, xp * 2 + core),
            )

    packed(right_s, serial[...])
    packed(right_m, mixed[...])

    wait(others(recv_b), recv_sems.at[3])
    each_region(lambda p: send(send_c.at[p], recv_c.at[r], 4, (p, g)))
    recv_c[r] = send_c[r]
    g_serial = dot_nn(q_t[...], recv_b[...].reshape(REGIONS * CAP, WIDTH)).astype(BF)
    g_serial_t[...] = g_serial.T
    to_sibling(unit_pairs(g_serial_t[...], True), right_m, 4 * CHUNK, 256, 4)

    scaled = (
        dot_nn(wproj[...], g_serial_t[...]).reshape(32, HEAD_DIM, PTS) * inv_sum
    ).astype(BF)
    grad_x[:, 0:128, :] = scaled.reshape(4, 128, PTS)
    gm[...] = scaled.reshape(WIDTH, PTS).T
    inner = -jnp.sum(scaled.astype(F32) * mixed_f[...], axis=1, keepdims=True)
    first = inner.astype(BF).astype(F32)
    second = (inner - first).astype(BF).astype(F32)
    third = inner - first - second
    place = lax.broadcasted_iota(jnp.int32, (32, HEAD_DIM, PTS), 1)
    terms = jnp.where(
        place == 0, first, jnp.where(place == 1, second, jnp.where(place == 2, third, 0.0))
    )
    grad_x[:, 128:256, :] = terms.astype(BF).reshape(4, 128, PTS)

    def backward(chunk, carry):
        col = pl.multiple_of(chunk * 128, 128)
        values = qkv[:, pl.ds(2 * WIDTH + col, 128)]
        grads = gm[:, pl.ds(col, 128)]
        queries = qs[:, pl.ds(col, 128)]
        spans = [slice(PTS * h, PTS * (h + 1)) for h in range(8)]
        for h in range(8):
            stack_g[spans[h], :] = grads * head_mask(h)
            stack_q[spans[h], :] = queries * head_mask(h)
        for h in range(8):
            chosen = jnp.where(
                (lane_1 // HEAD_DIM == h) & (lane_1 % HEAD_DIM < 3), 1.0, 0.0
            ).astype(BF)
            lhs = jnp.concatenate(
                [values * head_mask(h), jnp.broadcast_to(chosen, (PTS, 128))], axis=1
            )
            ds = dot_nn(lhs, grad_x[chunk]).astype(BF) * es[chunk, :, spans[h]]
            big_d[:, spans[h]] = ds
        for h in range(8):
            rows = pl.ds(pl.multiple_of(col + HEAD_DIM * h, HEAD_DIM), HEAD_DIM)
            left[HEAD_DIM * h : HEAD_DIM * (h + 1), :] = (
                dot_nn(kt[rows, :], big_d[:, spans[h]]) * 0.25
            ).astype(BF)
        gqkv[:, pl.ds(col, 128)] = left[0:128, :].T
        gk = dot_nn(big_d[...], stack_q[...]).astype(BF)
        gqkv[:, pl.ds(WIDTH + col, 128)] = gk
        left[128:256, :] = gk.T
        gv = dot_nn(es[chunk], stack_g[...]).astype(BF)
        gqkv[:, pl.ds(2 * WIDTH + col, 128)] = gv
        left[256:384, :] = gv.T
        base = pl.multiple_of(chunk * CHUNK, 64)
        to_sibling(unit_pairs(left[...], False), right_s, base, CHUNK, chunk)

        @pl.when(chunk == 0)
        def _():
            to_chips(4 * CHUNK, 256, 4)

        @pl.when(chunk > 0)
        def _():
            to_chips(pl.multiple_of((chunk - 1) * CHUNK, 64), CHUNK, chunk - 1)

        return carry

    lax.fori_loop(0, 4, backward, 0)

    grad_in = dot_nt(gqkv[...], wqkv[...]).astype(BF)
    send_d[...] = dot_nn(q_n[...], grad_in).astype(BF).reshape(REGIONS, CAP, WIDTH)
    each_region(lambda p: send(send_d.at[p], recv_d.at[r], 7, (p, g)))
    recv_d[r] = send_d[r]
    to_chips(3 * CHUNK, CHUNK, 3)
    grad_f = grad_in.astype(F32)
    store_rows(gs1, g, 0, jnp.sum(grad_f, axis=0, keepdims=True))
    store_rows(gs1, g, 4, jnp.sum(grad_f * unit_s[...], axis=0, keepdims=True))
    each_group(lambda p: send(gs1.at[g], gs1.at[g], 6, (r, p)))

    def gather_chips(at, rows, slot):
        wait(r_x.at[pl.ds(0, 3), pl.ds(at, rows)], x_recv.at[slot])
        span = slice(at, at + rows)
        mine = pl.ds(pl.multiple_of(xx * 128, 128), 128)
        total = own[span, mine] + r_core[span, mine].astype(F32)
        for k in range(1, 4):
            total = total + r_x[lax.rem(xx + k, 4), span, :].astype(F32)
        return total.astype(BF)

    def to_y(at, owner, row, slot):
        remote(
            s_y.at[pl.ds(at, 64)], r_y.at[yy, pl.ds(row, 64)], y_send.at[0], y_recv.at[slot],
            (owner * ZS + zz, g),
        )

    def chunk_to_y(j):
        total = gather_chips(j * CHUNK, CHUNK, j)
        for p in range(3):
            b = p * 4 + j
            s_y[64 * b : 64 * (b + 1), :] = total[64 * p : 64 * (p + 1), :]

            @pl.when(yy != b // 3)
            def _():
                to_y(64 * b, b // 3, 64 * (b % 3), b % 3)

    s_y[768:1024, :] = gather_chips(4 * CHUNK, 256, 4)
    for k in range(1, YS):
        yp = lax.rem(yy + k, YS)
        to_y(pl.multiple_of(768 + yp * 64, 64), yp, 192, 3)
    chunk_to_y(0)

    chunk_to_y(1)


    chunk_to_y(2)
    wait(others(gs1), recv_sems.at[6])
    gs2[yy] = jnp.sum(gs1[...], axis=0)
    along_y(gs2, 8)
    chunk_to_y(3)
    for m in range(3):
        at = pl.multiple_of((yy * 3 + m) * 64, 64)
        r_y[yy, 64 * m : 64 * (m + 1), :] = s_y[pl.ds(at, 64), :]
    r_y[yy, 192:256, :] = s_y[pl.ds(pl.multiple_of(768 + yy * 64, 64), 64), :]
    for slot in range(4):
        wait(r_y.at[pl.ds(0, 3), pl.ds(64 * slot, 64)], y_recv.at[slot])
    over_y = jnp.sum(r_y[...].astype(F32), axis=0).astype(BF)
    low = low_lanes[:, 0:128]

    def rows_of(unit):
        return over_y[16 * unit : 16 * (unit + 1), :]

    for z in range(ZS):
        half = z // 2
        middle, proj = rows_of(3 * half + 1).astype(F32), rows_of(12 + half).astype(F32)
        s_z[z, 0:16, :] = rows_of(3 * half + 2 * (z % 2))
        mixed_rows = jnp.where(low, proj, middle) if z % 2 else jnp.where(low, middle, proj)
        s_z[z, 16:32, :] = mixed_rows.astype(BF)
    for k in range(1, ZS):
        zp = lax.rem(zz + k, ZS)
        send(s_z.at[zp], r_z.at[zz], 10, (yy * ZS + zp, g))
    r_z[zz] = s_z[zz]
    wait(others(gs2), recv_sems.at[8])
    gs3[zz] = jnp.sum(gs2[...], axis=0)
    along_z(gs3, 5)

    wait(others(recv_c), recv_sems.at[4])
    out_ref[...] = dot_nn(p_t[...], recv_c[...].reshape(REGIONS * CAP, WIDTH)).astype(BF)

    wait(others(recv_d), recv_sems.at[7])
    grad_n = dot_nn(p_t[...], recv_d[...].reshape(REGIONS * CAP, WIDTH))
    scaled_n = grad_n * (inv_std * gain)
    unit_b = (x_ref[...].astype(F32) - mean_all) * inv_std

    wait(others(gs3), recv_sems.at[5])
    sums = jnp.sum(gs3[...], axis=0)
    grad_bias = load_row(sums, 0)
    grad_gain = load_row(sums, 4)
    gb_ref[...] = grad_bias
    gg_ref[...] = grad_gain
    scale = inv_std * gain * (1.0 / TOTAL)
    gp_ref[...] = (scaled_n - scale * grad_bias - unit_b * (scale * grad_gain)).astype(BF)

    wait(others(r_z), recv_sems.at[10])
    final = jnp.sum(r_z[...].astype(F32), axis=0)
    even = zz % 2 == 0
    a, b = final[0:16, 0:64], final[0:16, 64:128]
    c, d = final[16:32, 0:64], final[16:32, 64:128]
    gwq_ref[0:16, :] = jnp.where(even, a, d)
    gwq_ref[16:32, :] = jnp.where(even, b, a)
    gwq_ref[32:48, :] = jnp.where(even, c, b)
    gwp_ref[...] = jnp.where(even, d, c)

    for buf, stage in (
        (st1, 0), (send_a, 1), (st2, 2), (send_b, 3), (send_c, 4), (gs3, 5), (gs1, 6),
        (send_d, 7), (gs2, 8), (st3, 9), (r_z, 10),
    ):
        wait(others(buf), send_sems.at[stage])
    wait(s_y.at[pl.ds(0, 768)], y_send.at[0])
    for slot, at, rows in [(j, j * CHUNK, CHUNK) for j in range(4)] + [(4, 4 * CHUNK, 256)]:
        wait(g_core.at[pl.ds(at, rows)], core_send.at[slot])
        wait(s_x.at[pl.ds(0, 3), pl.ds(at, rows)], x_send.at[slot])


def deliver(*refs):
    n = len(refs) // 2
    sems = refs[-1]
    copies = [pltpu.make_async_copy(refs[i], refs[n + i], sems.at[i]) for i in range(n)]
    for copy in copies:
        copy.start()
    for copy in copies:
        copy.wait()


def on_device(points, row_slot, pos_slot, patch_ids, bn_gain, bn_bias, w_qkv, w_proj, cotangent):
    vmem = pl.BlockSpec(memory_space=pltpu.VMEM)
    hbm = pl.BlockSpec(memory_space=pltpu.HBM)
    args = tuple(pltpu.with_memory_space_constraint(a, pltpu.HBM) for a in (
        points[0], row_slot, pos_slot, patch_ids[0], bn_gain[None], bn_bias[None],
        w_qkv, w_proj, cotangent[0],
    ))

    def buf(dtype, *shape):
        return pltpu.VMEM(shape, dtype)

    scratch = [buf(a.dtype, *a.shape) for a in args]
    scratch += [pltpu.SemaphoreType.DMA((9,))]
    scratch += [buf(BF, REGIONS, CAP, WIDTH) for _ in range(8)]
    scratch += [buf(F32, n, 8, 128) for n in (GROUPS, YS, ZS, GROUPS, YS, ZS)]
    scratch += [
        buf(BF, PTS, WIDTH),
        buf(BF, WIDTH, PTS),
        buf(BF, PTS, WIDTH),
        buf(BF, PTS, 128),
        buf(BF, 4, 256, PTS),
        buf(BF, 4, 256, PTS),
        buf(F32, PTS, WIDTH),
        buf(BF, PTS, WIDTH),
        buf(BF, PTS, 3 * WIDTH),
        buf(BF, PTS, WIDTH),
        buf(BF, WIDTH, PTS),
        buf(BF, 32, 2 * HEAD_DIM, PTS),
        buf(F32, 8, PTS, PTS),
        buf(BF, 4, PTS, 8 * PTS),
        buf(F32, 32, 2 * HEAD_DIM, PTS),
        buf(F32, 32, HEAD_DIM, PTS),
        buf(BF, WIDTH, PTS),
        buf(BF, PTS, WIDTH),
        buf(BF, WIDTH, PTS),
        buf(BF, PTS, WIDTH),
        buf(BF, PTS, 8 * PTS),
        buf(BF, 8 * PTS, 128),
        buf(BF, 8 * PTS, 128),
        buf(BF, PTS, 3 * WIDTH),
        buf(BF, 384, PTS),
        buf(BF, 2, 2 * PTS, WIDTH),
        buf(BF, 2, 2 * PTS, WIDTH),
        buf(F32, 1024, WIDTH),
        buf(BF, 1024, WIDTH),
        buf(BF, 1024, WIDTH),
        buf(BF, 4, 1024, 128),
        buf(BF, 4, 1024, 128),
        buf(BF, 1024, 128),
        buf(BF, YS, 256, 128),
        buf(BF, ZS, 32, 128),
        buf(BF, ZS, 32, 128),
    ]
    scratch += [pltpu.SemaphoreType.DMA((n,)) for n in (11, 11, 5, 5, 5, 5, 1, 4)]
    shapes = [
        jax.ShapeDtypeStruct((PTS, WIDTH), BF),
        jax.ShapeDtypeStruct((PTS, WIDTH), BF),
        jax.ShapeDtypeStruct((48, 64), F32),
        jax.ShapeDtypeStruct((16, 64), F32),
        jax.ShapeDtypeStruct((1, WIDTH), F32),
        jax.ShapeDtypeStruct((1, WIDTH), F32),
    ]
    results = pl.pallas_call(
        kernel,
        out_shape=shapes,
        in_specs=[hbm] * 9,
        out_specs=[vmem] * 6,
        scratch_shapes=scratch,
        compiler_params=pltpu.CompilerParams(
            collective_id=0, has_side_effects=True, vmem_limit_bytes=52 * 1024 * 1024
        ),
    )(*args)
    output, grad_points, grad_qkv, grad_proj, grad_gain, grad_bias = pl.pallas_call(
        deliver,
        out_shape=shapes,
        in_specs=[pl.BlockSpec(memory_space=pl.ANY)] * 6,
        out_specs=[hbm] * 6,
        scratch_shapes=[pltpu.SemaphoreType.DMA((6,))],
        compiler_params=pltpu.CompilerParams(vmem_limit_bytes=4 * 1024 * 1024),
    )(*results)
    return output[None], grad_points[None], grad_qkv.T, grad_proj.T, grad_gain[0], grad_bias[0]


def solution(mesh):
    placed = (
        P("group", "region", None),
        P("group", "region"),
        P("group", "region"),
        P("group", "region", None),
        P(),
        P(),
        P(),
        P(),
        P("group", "region", None),
    )
    return jax.shard_map(
        on_device,
        mesh=mesh,
        in_specs=placed,
        out_specs=(
            P("group", "region", None),
            P("group", "region", None),
            P("group", "region"),
            P("group", "region"),
            P(),
            P(),
        ),
        check_vma=False,
    )
```
